32 devices in a mesh: dp: 8 (over y, x, core), mp: 4 (over z).
Axes of the slice: x: 2, y: 2, z: 4, core: 2. Of those that a mesh axis runs over, the one named last changes fastest.
Arguments:
- tokens: bfloat16 [8192, 1024], P('dp'), may hold values from -6 to 6
- lengths: int32 [8], P('dp'), may hold values from 1 to 1024, as said below
- w_qkv: float32 [1024, 3072], P('dp'), may hold values from -0.1875 to 0.1875
- w_out: float32 [1024, 1024], P('dp'), may hold values from -1 to 1
- ln1_gain: float32 [1024], P('dp'), may hold values from 0.5 to 1.5
- ln2_gain: float32 [1024], P('dp'), may hold values from 0.5 to 1.5
- w_in: float32 [1024, 4096], P('dp', 'mp'), may hold values from -0.1875 to 0.1875
- b_in: float32 [4096], P(('mp', 'dp')), may hold values from -3 to 3
- w_back: float32 [4096, 1024], P('mp', 'dp'), may hold values from -0.09375 to 0.09375
- b_back: float32 [1024], P('dp'), may hold values from -2 to 2
- cotangent: bfloat16 [8192, 1024], P('dp'), may hold values from -6 to 6
Outputs:
- output: bfloat16 [8192, 1024], P('dp')
- grad_tokens: float32 [8192, 1024], P('dp')
- grad_w_qkv: float32 [1024, 3072], P('dp')
- grad_w_out: float32 [1024, 1024], P('dp')
- grad_ln1_gain: float32 [1024], P('dp')
- grad_ln2_gain: float32 [1024], P('dp')
- grad_w_in: float32 [1024, 4096], P('dp', 'mp')
- grad_b_in: float32 [4096], P(('mp', 'dp'))
- grad_w_back: float32 [4096, 1024], P('mp', 'dp')
- grad_b_back: float32 [1024], P('dp')
The draws below stay inside these ranges and needn't reach their ends.
Inputs may be any that keep to these rules, and one draw needn't show every extreme that they name: `lengths`: each image's pixels fill the start of its slot of 1024 rows; every index of dp holds at least one image of exactly 1024 pixels.
All inputs are finite; a program needn't handle non-finite values.
Results may differ from the reference program's by a relative error of at most 0.012.
Values may be sent and summed in bfloat16 or wider, within the bound.
No kernel may reach another device: no remote copies, remote signals or barrier semaphores. Data moves between devices by JAX's collectives and lax.ppermute only.
A program may use at most 192 MiB of HBM per device.

```python
import math
import jax
import jax.numpy as jnp
from jax import lax

D = 1024
H = 16
HD = 64
FF = 4096
SEQ = 1024
BLOCK = 512
SLOTS = 1
IMAGES = 8
TOKENS = 8192
N_DP = 8


def draw_lengths(key, part):
    key = jax.random.fold_in(key, 17)
    first_key, second_key = jax.random.split(key, 2)
    picks = jax.random.randint(first_key, (IMAGES, 3), 0, SEQ)
    shortened = picks[:, 0] * picks[:, 1] // SEQ
    shortened = shortened * picks[:, 2] // SEQ
    kept = (SEQ - shortened).reshape(N_DP, SLOTS)
    chosen = jax.random.randint(second_key, (N_DP, 1), 0, SLOTS)
    whole_image = jnp.arange(SLOTS)[None, :] == chosen
    return jnp.where(whole_image, SEQ, kept).reshape(IMAGES).astype(jnp.int32)


def levels(rng, dims, shards, smallest, top_value):
    def one(dim, shards_of):
        steps = jax.random.uniform(jax.random.fold_in(jax.random.fold_in(rng, 6), dim), (shards_of,), jnp.float32, smallest / len(shards), top_value / len(shards))
        return jnp.repeat(jnp.exp(steps), dims[dim] // shards_of).reshape((-1,) + (1,) * (len(dims) - dim - 1))

    factor_of = one(*shards[0])
    for cut in shards[1:]:
        factor_of = factor_of * one(*cut)
    return factor_of


def bell_draw(rng, extent, scale, most, cuts=(), held_as=jnp.bfloat16):
    entries = jax.random.normal(rng, extent, jnp.float32) * scale
    if len(cuts) > 0:
        entries = levels(rng, extent, cuts, -0.22, 0.18) * entries
    return jnp.clip(entries, min=-most, max=most).astype(held_as)


def setup_inputs(seed: int = 0) -> dict:
    seeds = jax.random.split(jax.random.key(seed), 12)
    return {
        "tokens": bell_draw(seeds[0], (TOKENS, D), 1.0, 6.0, ((0, 8),)),
        "lengths": draw_lengths(jax.random.fold_in(seeds[11], 71), 0),
        "w_qkv": bell_draw(seeds[2], (D, 3 * D), D ** -0.5, 0.1875, ((0, 8),), jnp.float32),
        "w_out": bell_draw(seeds[3], (D, D), (D // 32) ** -0.5, 1.0, ((0, 8),), jnp.float32),
        "ln1_gain": jnp.clip(1.0 + 0.1 * jax.random.normal(seeds[4], (D,), jnp.float32), 0.5, 1.5),
        "ln2_gain": jnp.clip(1.0 + 0.1 * jax.random.normal(seeds[5], (D,), jnp.float32), 0.5, 1.5),
        "w_in": bell_draw(seeds[6], (D, FF), D ** -0.5, 0.1875, ((0, 8), (1, 4)), jnp.float32),
        "b_in": bell_draw(seeds[7], (FF,), 0.5, 3.0, ((0, 32),), jnp.float32),
        "w_back": bell_draw(seeds[8], (FF, D), FF ** -0.5, 0.09375, ((0, 4), (1, 8)), jnp.float32),
        "b_back": bell_draw(seeds[9], (D,), 0.3, 2.0, ((0, 8),), jnp.float32),
        "cotangent": bell_draw(seeds[10], (TOKENS, D), 1.0, 6.0, ((0, 8),)),
    }


highest = lax.Precision.HIGHEST
epsilon = 1e-05

@jax.custom_vjp
def low(v):
    return lax.optimization_barrier(v.astype(jnp.bfloat16)).astype(jnp.float32)

@jax.custom_vjp
def low_back(v):
    return v

def low_keep(v):
    return (low(v), None)

def low_pass(kept, grad):
    return (grad,)

def back_keep(v):
    return (v, None)

def back_low(kept, grad):
    return (low(grad),)
low.defvjp(low_keep, low_pass)
low_back.defvjp(back_keep, back_low)

def normalize(values):
    centre = lax.optimization_barrier(jnp.mean(values, -1, keepdims=True))
    centred = values - centre
    spread = lax.optimization_barrier(jnp.mean(centred * centred, -1, keepdims=True))
    return centred * lax.rsqrt(spread + epsilon)

def reference(tokens, lengths, w_qkv, w_out, ln1_gain, ln2_gain, w_in, b_in, w_back, b_back, cotangent):
    position = jnp.arange(TOKENS, dtype=jnp.int32) % SEQ
    limit = jnp.repeat(lengths, SEQ, total_repeat_length=TOKENS)
    keep_rows = (position < limit).astype(jnp.float32)[:, None]
    group_images = math.gcd(IMAGES, max(1, 4096 // SEQ))
    block_count = SEQ // BLOCK
    causal = (jnp.arange(BLOCK)[:, None] >= jnp.arange(BLOCK)[None, :]).astype(jnp.float32)

    def forward(inputs, w_attn, w_mix, gain_one, gain_two, w_up, bias_up, w_down, bias_down):
        attn_low = low(w_attn)
        mix_low = low(w_mix)
        up_low = low(w_up)
        down_low = low(w_down)

        def one_group(pieces):
            x_group, keep_group = pieces
            group_rows = x_group.shape[0]
            attn_in = low(normalize(x_group) * gain_one)
            projected = low_back(jnp.dot(attn_in, attn_low, precision=highest))
            query = projected[:, :D].reshape(group_rows, H, HD)
            keys = projected[:, D:2 * D].reshape(group_rows, H, HD)
            values = projected[:, 2 * D:].reshape(group_rows, H, HD)
            feat_q = low(jax.nn.elu(query) + 1.0)
            feat_k = low(jax.nn.elu(keys) + 1.0)
            values_aug = jnp.concatenate([low(values), jnp.ones((group_rows, H, 1), jnp.float32)], -1)

            def split_blocks(arr):
                return jnp.swapaxes(arr.reshape(group_images, block_count, BLOCK, H, arr.shape[-1]), 0, 1)

            def block_step(state, blk):
                q_blk, k_blk, v_blk = blk
                scores = jnp.einsum('gqhd,gkhd->ghqk', q_blk, k_blk, precision=highest) * causal
                weights = low(low_back(scores))
                augmented = jnp.einsum('ghqk,gkhe->gqhe', weights, v_blk, precision=highest)
                augmented = augmented + jnp.einsum('gqhd,ghde->gqhe', q_blk, state, precision=highest)
                state = state + jnp.einsum('gkhd,gkhe->ghde', k_blk, v_blk, precision=highest)
                return (state, augmented)
            start_state = jnp.zeros((group_images, H, HD, HD + 1), jnp.float32)
            _, augmented = lax.scan(jax.checkpoint(block_step), start_state, (split_blocks(feat_q), split_blocks(feat_k), split_blocks(values_aug)))
            augmented = jnp.swapaxes(augmented, 0, 1).reshape(group_rows, H, HD + 1)
            numer = low_back(augmented[..., :HD])
            denom = low_back(augmented[..., HD:])
            att_low = low((numer / denom).reshape(group_rows, D))
            resid = x_group + low_back(jnp.dot(att_low, mix_low, precision=highest))
            mlp_in = low(normalize(resid) * gain_two)
            hidden_pre = low_back(jnp.dot(mlp_in, up_low, precision=highest) + bias_up)
            hidden = low(jax.nn.gelu(hidden_pre))
            mlp_out = jnp.dot(hidden, down_low, precision=highest) + bias_down
            return (resid + mlp_out) * keep_group
        groups = IMAGES // group_images
        result = lax.map(jax.checkpoint(one_group), (inputs.reshape(groups, group_images * SEQ, D), keep_rows.reshape(groups, group_images * SEQ, 1)))
        return result.reshape(TOKENS, D)
    output, pull = jax.vjp(forward, tokens.astype(jnp.float32), w_qkv, w_out, ln1_gain, ln2_gain, w_in, b_in, w_back, b_back)
    grads = pull(cotangent.astype(jnp.float32))
    return (output.astype(jnp.bfloat16), grads[0], grads[1], grads[2], grads[3], grads[4], grads[5], grads[6], grads[7], grads[8])
```

```python
import functools

import jax
import jax.numpy as jnp
from jax import lax
from jax.experimental import pallas as pl
from jax.experimental.pallas import tpu as pltpu
from jax.sharding import PartitionSpec as P

HD = 64
PAIR = 2 * HD
CHUNK = 256
EPS = 1e-05
PAIRED = 8
F32 = jnp.float32
BF16 = jnp.bfloat16
VMEM_LIMIT = 60 * 1024 * 1024
GELU_A = 0.7978845608028654
GELU_B = 0.044715

ANY = pl.BlockSpec(memory_space=pl.ANY)
SMEM = pl.BlockSpec(memory_space=pltpu.SMEM)
VMEM = pl.BlockSpec(memory_space=pltpu.VMEM)


def nn(left, right):
    return jnp.dot(left, right, preferred_element_type=F32)


def nt(left, right):
    return lax.dot_general(left, right, (((1,), (1,)), ((), ())), preferred_element_type=F32)


def tn(left, right):
    return lax.dot_general(left, right, (((0,), (0,)), ((), ())), preferred_element_type=F32)


def normalize(values):
    centre = jnp.mean(values, -1, keepdims=True)
    centred = values - centre
    spread = jnp.mean(centred * centred, -1, keepdims=True)
    factor = lax.rsqrt(spread + EPS)
    return centred * factor, factor


def norm_back(grad, normed, factor):
    return factor * (
        grad
        - jnp.mean(grad, -1, keepdims=True)
        - normed * jnp.mean(grad * normed, -1, keepdims=True)
    )


def start_pieces(base, pieces, dst, sems, axis):
    copies = []
    size = dst.shape[axis] // len(pieces)
    for k, piece in enumerate(pieces):
        at = pl.multiple_of((base ^ k) * size, size) if len(pieces) > 1 else 0
        view = dst.at[pl.ds(at, size)] if axis == 0 else dst.at[:, pl.ds(at, size)]
        copy = pltpu.make_async_copy(piece, view, sems.at[k])
        copy.start()
        copies.append(copy)
    return copies


def keep_of(length, start, rows):
    position = lax.broadcasted_iota(jnp.int32, (rows, 1), 0) + start
    return (position < length).astype(F32)


def lane_masks():
    lane = lax.broadcasted_iota(jnp.int32, (CHUNK, PAIR), 1)
    first = (lane < HD).astype(F32)
    return first.astype(BF16), (1.0 - first).astype(BF16)


def block_mask():
    row = lax.broadcasted_iota(jnp.int32, (PAIR, 2 * PAIR), 0)
    col = lax.broadcasted_iota(jnp.int32, (PAIR, 2 * PAIR), 1)
    return ((row < HD) == (col < PAIR)).astype(F32)


def split(state):
    high = state.astype(BF16)
    return high, (state - high.astype(F32)).astype(BF16)


def pair_of(arr, p):
    return arr[:, p * PAIR : (p + 1) * PAIR]


def attn_fwd_kernel(n_pieces, meta, attn_in, *refs):
    pieces = refs[:n_pieces]
    fq_out, fk_out, val_out, att_out, rden_out, weight, sems = refs[n_pieces:]
    for copy in start_pieces(meta[0], pieces, weight, sems, 0):
        copy.wait()
    rows_all = attn_in.shape[0]
    width = fq_out.shape[1]
    pairs = width // PAIR
    mask_a, mask_b = lane_masks()
    blocks = block_mask()
    first = lax.broadcasted_iota(jnp.int32, (CHUNK, PAIR), 1) < HD
    causal = lax.broadcasted_iota(jnp.int32, (CHUNK, CHUNK), 0) >= lax.broadcasted_iota(
        jnp.int32, (CHUNK, CHUNK), 1
    )
    states = [jnp.zeros((PAIR, 2 * PAIR), F32) for _ in range(pairs)]
    count = rows_all // CHUNK
    for c in range(count):
        rows = pl.ds(c * CHUNK, CHUNK)
        proj = nn(attn_in[rows, :], weight[...])
        query, keys = proj[:, :width], proj[:, width : 2 * width]
        fq = jnp.where(query > 0, query + 1.0, jnp.exp(jnp.minimum(query, 0.0))).astype(BF16)
        fk = jnp.where(keys > 0, keys + 1.0, jnp.exp(jnp.minimum(keys, 0.0))).astype(BF16)
        val = proj[:, 2 * width :].astype(BF16)
        fq_out[rows, :] = fq
        fk_out[rows, :] = fk
        val_out[rows, :] = val
        for p in range(pairs):
            q, k, v = pair_of(fq, p), pair_of(fk, p), pair_of(val, p)
            v_a = v * mask_a + mask_b
            v_b = v * mask_b + mask_a
            s_a = jnp.where(causal, nt(q * mask_a, k), 0.0).astype(BF16)
            s_b = jnp.where(causal, nt(q * mask_b, k), 0.0).astype(BF16)
            r_a = nn(s_a, v_a)
            r_b = nn(s_b, v_b)
            if c > 0:
                high, low = split(states[p])
                past = nn(q, high) + nn(q, low)
                r_a = r_a + past[:, :PAIR]
                r_b = r_b + past[:, PAIR:]
            numer = jnp.where(first, r_a, r_b)
            denom = pltpu.roll(jnp.where(first, r_b, r_a), HD, axis=1)
            inverse = 1.0 / denom
            cols = pl.ds(p * PAIR, PAIR)
            att_out[rows, cols] = (numer * inverse).astype(BF16)
            rden_out[rows, cols] = inverse
            if c + 1 < count:
                states[p] = states[p] + tn(k, jnp.concatenate([v_a, v_b], 1)) * blocks


def attn_fwd(meta, attn_in, pieces):
    rows, width = attn_in.shape[0], pieces[0].shape[1] // 3
    n = len(pieces)
    low = jax.ShapeDtypeStruct((rows, width), BF16)
    return pl.pallas_call(
        functools.partial(attn_fwd_kernel, n),
        out_shape=(low, low, low, low, jax.ShapeDtypeStruct((rows, width), F32)),
        in_specs=[SMEM, VMEM] + [ANY] * n,
        out_specs=(VMEM,) * 5,
        scratch_shapes=[
            pltpu.VMEM((attn_in.shape[1], 3 * width), BF16),
            pltpu.SemaphoreType.DMA((n,)),
        ],
        compiler_params=pltpu.CompilerParams(vmem_limit_bytes=VMEM_LIMIT),
        cost_estimate=pl.CostEstimate(
            flops=rows * 1024 * 3 * width * 4, bytes_accessed=rows * 1024 * 8, transcendentals=0
        ),
        name="attn_fwd",
    )(meta, attn_in, *pieces)


def mlp_kernel(n_pieces, groups, start, meta, *refs):
    atts = refs[:groups]
    tok, cot, gain, bias = refs[groups : groups + 4]
    refs = refs[groups + 4 :]
    pieces_o, pieces_i, pieces_b = (refs[a * n_pieces : (a + 1) * n_pieces] for a in range(3))
    refs = refs[3 * n_pieces :]
    gn_out, hidden_out, gpre_out, min_out, resid_out = refs[:5]
    w_o, w_i, w_b, sems = refs[5:]
    waits = [
        start_pieces(meta[0], pieces, dst, sems.at[a], axis)
        for a, (pieces, dst, axis) in enumerate(
            ((pieces_o, w_o, 0), (pieces_i, w_i, 0), (pieces_b, w_b, 1))
        )
    ]
    width = atts[0].shape[1]
    rows_all = tok.shape[0]
    for c in range(rows_all // CHUNK):
        rows = pl.ds(c * CHUNK, CHUNK)
        if c == 0:
            for copy in waits[0]:
                copy.wait()
        mixed = None
        for j in range(groups):
            at = pl.multiple_of(lax.rem(meta[1] + j, groups) * width, width)
            part = nn(atts[j][rows, :], w_o[pl.ds(at, width), :])
            mixed = part if mixed is None else mixed + part
        resid = tok[rows, :].astype(F32) + mixed
        resid_out[rows, :] = resid
        normed, _ = normalize(resid)
        mlp_in = (normed * gain[...]).astype(BF16)
        min_out[rows, :] = mlp_in
        if c == 0:
            for copy in waits[1]:
                copy.wait()
        pre = nn(mlp_in, w_i[...]) + bias[...]
        square = pre * pre
        t = jnp.tanh(GELU_A * pre * (1.0 + GELU_B * square))
        half = 0.5 * (1.0 + t)
        hidden_out[rows, :] = (pre * half).astype(BF16)
        slope = half + (0.5 * GELU_A) * pre * (1.0 - t * t) * (1.0 + (3.0 * GELU_B) * square)
        keep = keep_of(meta[2], start + c * CHUNK, CHUNK)
        g_low = (cot[rows, :].astype(F32) * keep).astype(BF16)
        if c == 0:
            for copy in waits[2]:
                copy.wait()
        gpre = (nt(g_low, w_b[...]) * slope).astype(BF16)
        gpre_out[rows, :] = gpre
        gn_out[rows, :] = nt(gpre, w_i[...]).astype(BF16)


def mlp(meta, start, rows, atts, tokens, cotangent, gain, bias, p_out, p_in, p_back):
    n, groups = len(p_out), len(atts)
    width = tokens.shape[1]
    hidden = bias.shape[1]
    block = start // rows

    def rowed(arr):
        return pl.BlockSpec((rows, arr.shape[1]), lambda i: (block, 0))

    def whole(shape):
        return pl.BlockSpec(shape, lambda i: (0, 0))

    def low(cols):
        return jax.ShapeDtypeStruct((rows, cols), BF16)

    return pl.pallas_call(
        functools.partial(mlp_kernel, n, groups, start),
        grid=(1,),
        out_shape=(
            low(width),
            low(hidden),
            low(hidden),
            low(width),
            jax.ShapeDtypeStruct((rows, width), F32),
        ),
        in_specs=[SMEM]
        + [rowed(a) for a in atts]
        + [rowed(tokens), rowed(cotangent), whole(gain.shape), whole(bias.shape)]
        + [ANY] * (3 * n),
        out_specs=(
            whole((rows, width)),
            whole((rows, hidden)),
            whole((rows, hidden)),
            whole((rows, width)),
            whole((rows, width)),
        ),
        scratch_shapes=[
            pltpu.VMEM((width, width), BF16),
            pltpu.VMEM((width, hidden), BF16),
            pltpu.VMEM((hidden, width), BF16),
            pltpu.SemaphoreType.DMA((3, n)),
        ],
        compiler_params=pltpu.CompilerParams(vmem_limit_bytes=VMEM_LIMIT),
        cost_estimate=pl.CostEstimate(
            flops=rows * 1024 * 1024 * 8 * 2, bytes_accessed=rows * 1024 * 16, transcendentals=0
        ),
        name="mlp_fwd_bwd",
    )(meta, *atts, tokens, cotangent, gain, bias, *p_out, *p_in, *p_back)


def mlp_out_kernel(n_pieces, parts, meta, *refs):
    hiddens = refs[:parts]
    pieces = refs[parts : parts + n_pieces]
    outs = refs[parts + n_pieces : 2 * parts + n_pieces]
    w_b, sems = refs[2 * parts + n_pieces :]
    for copy in start_pieces(meta[0], pieces, w_b, sems, 1):
        copy.wait()
    for hidden, out in zip(hiddens, outs):
        for c in range(hidden.shape[0] // CHUNK):
            rows = pl.ds(c * CHUNK, CHUNK)
            out[rows, :] = nn(hidden[rows, :], w_b[...]).astype(BF16)


def mlp_out(meta, hiddens, p_back):
    n, parts = len(p_back), len(hiddens)
    rows, hidden = hiddens[0].shape
    width = n * p_back[0].shape[1]
    return pl.pallas_call(
        functools.partial(mlp_out_kernel, n, parts),
        out_shape=(jax.ShapeDtypeStruct((rows, width), BF16),) * parts,
        in_specs=[SMEM] + [VMEM] * parts + [ANY] * n,
        out_specs=(VMEM,) * parts,
        scratch_shapes=[pltpu.VMEM((hidden, width), BF16), pltpu.SemaphoreType.DMA((n,))],
        compiler_params=pltpu.CompilerParams(vmem_limit_bytes=VMEM_LIMIT),
        cost_estimate=pl.CostEstimate(
            flops=2 * parts * rows * 1024 * 1024, bytes_accessed=rows * 1024 * 16, transcendentals=0
        ),
        name="mlp_out",
    )(meta, *hiddens, *p_back)


def offset_of(n_blocks, base, k, size):
    return pl.multiple_of((base ^ k) * size, size) if n_blocks == PAIRED else k * size


def mlp_grads_kernel(n_pieces, parts, meta, *refs):
    hiddens, gpres, mins = (refs[a * parts : (a + 1) * parts] for a in range(3))
    cot = refs[3 * parts]
    down_own, down_sib, up_own, up_sib, bin_out, bback_out, down, up, g_low = refs[3 * parts + 1 :]
    rows = hiddens[0].shape[0]
    base = meta[0]
    total_in = total_back = None
    for r in range(parts):
        keep = keep_of(meta[2], r * rows, rows)
        g = cot[pl.ds(r * rows, rows), :].astype(F32) * keep
        g_low[pl.ds(r * rows, rows), :] = g.astype(BF16)
        back = jnp.sum(g, 0, keepdims=True)
        inner = jnp.sum(gpres[r][...].astype(F32), 0, keepdims=True)
        total_in = inner if total_in is None else total_in + inner
        total_back = back if total_back is None else total_back + back
    bin_out[...] = total_in
    bback_out[...] = total_back
    step = 256

    def product(lefts, right_of, scratch):
        for s in range(scratch.shape[0] // step):
            total = None
            for r in range(parts):
                part = tn(lefts[r][:, s * step : (s + 1) * step], right_of(r))
                total = part if total is None else total + part
            scratch[pl.ds(s * step, step), :] = total.astype(BF16)

    product(hiddens, lambda r: g_low[pl.ds(r * rows, rows), :], down)
    size = down_own.shape[2]
    for k in range(n_pieces):
        at = offset_of(n_pieces, base, k, size)
        (down_own, down_sib)[k & 1][k >> 1] = down[:, pl.ds(at, size)]
    product(mins, lambda r: gpres[r][...], up)
    size = up_own.shape[1]
    for k in range(n_pieces):
        at = offset_of(n_pieces, base, k, size)
        (up_own, up_sib)[k & 1][k >> 1] = up[pl.ds(at, size), :]


def mlp_grads(meta, n_blocks, hiddens, gpres, mins, cotangent):
    parts = len(hiddens)
    hidden, width = hiddens[0].shape[1], mins[0].shape[1]
    down = jax.ShapeDtypeStruct((n_blocks // 2, hidden, width // n_blocks), BF16)
    up = jax.ShapeDtypeStruct((n_blocks // 2, width // n_blocks, hidden), BF16)
    return pl.pallas_call(
        functools.partial(mlp_grads_kernel, n_blocks, parts),
        out_shape=(
            down,
            down,
            up,
            up,
            jax.ShapeDtypeStruct((1, hidden), F32),
            jax.ShapeDtypeStruct((1, width), F32),
        ),
        in_specs=[SMEM] + [VMEM] * (3 * parts + 1),
        out_specs=(VMEM,) * 6,
        scratch_shapes=[
            pltpu.VMEM((hidden, width), BF16),
            pltpu.VMEM((width, hidden), BF16),
            pltpu.VMEM(cotangent.shape, BF16),
        ],
        compiler_params=pltpu.CompilerParams(vmem_limit_bytes=VMEM_LIMIT),
        cost_estimate=pl.CostEstimate(
            flops=8 * 1024 * 1024 * 1024, bytes_accessed=16 * 1024 * 1024, transcendentals=0
        ),
        name="mlp_grads",
    )(meta, *hiddens, *gpres, *mins, cotangent)


def attn_bwd_group(rows_all, width, w_o, grad_mix, fq, fk, val, att, rden, gproj, state_scr):
    pairs = width // PAIR
    count = rows_all // CHUNK
    mask_a, mask_b = lane_masks()
    blocks = block_mask()
    first = lax.broadcasted_iota(jnp.int32, (CHUNK, PAIR), 1) < HD
    row = lax.broadcasted_iota(jnp.int32, (CHUNK, CHUNK), 0)
    col = lax.broadcasted_iota(jnp.int32, (CHUNK, CHUNK), 1)
    causal, causal_t = row >= col, row <= col
    head_row = lax.broadcasted_iota(jnp.int32, (width, width), 0) // HD
    head_col = lax.broadcasted_iota(jnp.int32, (width, width), 1) // HD
    head_sum = (head_row == head_col).astype(F32).astype(BF16)

    states = [jnp.zeros((PAIR, 2 * PAIR), F32) for _ in range(pairs)]
    for c in range(count - 1):
        rows = pl.ds(c * CHUNK, CHUNK)
        for p in range(pairs):
            cols = pl.ds(p * PAIR, PAIR)
            k, v = fk[rows, cols], val[rows, cols]
            aug = jnp.concatenate([v * mask_a + mask_b, v * mask_b + mask_a], 1)
            states[p] = states[p] + tn(k, aug) * blocks
            high, low = split(states[p])
            state_scr[c + 1, p, 0] = high
            state_scr[c + 1, p, 1] = low

    later = [jnp.zeros((PAIR, 2 * PAIR), F32) for _ in range(pairs)]
    for c in reversed(range(count)):
        rows = pl.ds(c * CHUNK, CHUNK)
        grad_att = nt(grad_mix[rows, :], w_o[...])
        inverse = rden[rows, :]
        gnum = (grad_att * inverse).astype(BF16)
        dots = nn((grad_att * att[rows, :].astype(F32)).astype(BF16), head_sum)
        gden = (-dots * inverse).astype(BF16).astype(F32)
        for p in range(pairs):
            cols = pl.ds(p * PAIR, PAIR)
            q, k, v = fq[rows, cols], fk[rows, cols], val[rows, cols]
            num = pair_of(gnum, p)
            den = (pltpu.roll(pair_of(gden, p), HD, axis=1) * (1.0 / HD)).astype(BF16)
            n_a, n_b = num * mask_a + den * mask_b, num * mask_b + den * mask_a
            q_a, q_b = q * mask_a, q * mask_b
            v_a, v_b = v * mask_a + mask_b, v * mask_b + mask_a
            n_cat = jnp.concatenate([n_a, n_b], 1)
            v_cat = jnp.concatenate([v_a, v_b], 1)
            st_a = jnp.where(causal_t, nt(k, q_a), 0.0).astype(BF16)
            st_b = jnp.where(causal_t, nt(k, q_b), 0.0).astype(BF16)
            gs_a = jnp.where(causal, nt(n_a, v_a), 0.0).astype(BF16)
            gs_b = jnp.where(causal, nt(n_b, v_b), 0.0).astype(BF16)
            gt_a = jnp.where(causal_t, nt(v_a, n_a), 0.0).astype(BF16)
            gt_b = jnp.where(causal_t, nt(v_b, n_b), 0.0).astype(BF16)
            gq = nn(gs_a, k * mask_a) + nn(gs_b, k * mask_b)
            gk = nn(gt_a, q_a) + nn(gt_b, q_b)
            gv = nn(st_a, num * mask_a) + nn(st_b, num * mask_b)
            if c > 0:
                gq = gq + nt(n_cat, state_scr[c, p, 0]) + nt(n_cat, state_scr[c, p, 1])
            if c + 1 < count:
                high, low = split(later[p])
                gk = gk + nt(v_cat, high) + nt(v_cat, low)
                past = nn(k, high) + nn(k, low)
                gv = gv + jnp.where(first, past[:, :PAIR], past[:, PAIR:])
            if c > 0:
                later[p] = later[p] + tn(q, n_cat) * blocks
            gproj[rows, pl.ds(p * PAIR, PAIR)] = (
                gq * jnp.minimum(q.astype(F32), 1.0)
            ).astype(BF16)
            gproj[rows, pl.ds(width + p * PAIR, PAIR)] = (
                gk * jnp.minimum(k.astype(F32), 1.0)
            ).astype(BF16)
            gproj[rows, pl.ds(2 * width + p * PAIR, PAIR)] = gv.astype(BF16)


def start_group_rows(meta, group, width, pieces, dst, sems):
    copies = []
    size = pieces[0].shape[0]
    if len(pieces) == 1:
        copy = pltpu.make_async_copy(
            pieces[0].at[pl.ds(pl.multiple_of(group * width, width), width)], dst, sems.at[0]
        )
        copy.start()
        return [copy]
    for part in range(width // size):
        owner = group * (width // size) + part
        for k, piece in enumerate(pieces):
            @pl.when(owner == (meta[0] ^ k))
            def _():
                pltpu.make_async_copy(
                    piece, dst.at[pl.ds(part * size, size)], sems.at[part]
                ).start()
        copies.append(
            pltpu.make_async_copy(pieces[0], dst.at[pl.ds(part * size, size)], sems.at[part])
        )
    return copies


def mid_kernel(n_pieces, groups, n_totals, parts, n_blocks, meta, *refs):
    totals = refs[:n_totals]
    resids = refs[n_totals : n_totals + parts]
    cot, gain = refs[n_totals + parts : n_totals + parts + 2]
    refs = refs[n_totals + parts + 2 :]
    atts = refs[:groups]
    attn_in, fq, fk, val, rden = refs[groups : groups + 5]
    pieces = refs[groups + 5 : groups + 5 + n_pieces]
    refs = refs[groups + 5 + n_pieces :]
    gres_out, gmix_out, gain_out, gproj_out, wo_own, wo_sib, wq_own, wq_sib = refs[:8]
    w_o, state_scr, wo_scr, wq_scr, sems = refs[8:]
    width = fq.shape[1]
    rows_all = cot.shape[0]
    base, place = meta[0], meta[1]
    copies = start_group_rows(meta, place, width, pieces, w_o, sems)
    part_rows = resids[0].shape[0]
    total_rows = totals[0].shape[0]
    gain_sum = jnp.zeros(gain_out.shape, F32)
    for c in range(rows_all // CHUNK):
        rows = pl.ds(c * CHUNK, CHUNK)
        inner = (c * CHUNK) % part_rows
        resid = resids[c * CHUNK // part_rows][pl.ds(inner, CHUNK), :]
        inner = (c * CHUNK) % total_rows
        grad = totals[c * CHUNK // total_rows][pl.ds(inner, CHUNK), :].astype(F32)
        normed, factor = normalize(resid)
        gain_sum = gain_sum + jnp.sum(grad * normed, 0, keepdims=True)
        keep = keep_of(meta[2], c * CHUNK, CHUNK)
        gres = cot[rows, :].astype(F32) * keep + norm_back(grad * gain[...], normed, factor)
        gres_out[rows, :] = gres
        gmix_out[rows, :] = gres.astype(BF16)
    gain_out[...] = gain_sum

    cols = pl.ds(pl.multiple_of(place * width, width), width)
    g_cols = gmix_out[:, cols]
    for j in range(groups):
        at = pl.multiple_of(lax.rem(place + j, groups) * width, width)
        wo_scr[pl.ds(at, width), :] = tn(atts[j][...], g_cols).astype(BF16)
    size = wo_own.shape[1]
    for k in range(n_blocks):
        at = offset_of(n_blocks, base, k, size)
        (wo_own, wo_sib)[k & 1][k >> 1] = wo_scr[pl.ds(at, size), :]

    for copy in copies:
        copy.wait()
    attn_bwd_group(
        rows_all, width, w_o, gmix_out, fq, fk, val, atts[0], rden, gproj_out, state_scr
    )
    for s in range(attn_in.shape[1] // 256):
        wq_scr[pl.ds(s * 256, 256), :] = tn(
            attn_in[:, s * 256 : (s + 1) * 256], gproj_out[...]
        ).astype(BF16)
    size = wq_own.shape[1]
    for k in range(n_blocks):
        at = offset_of(n_blocks, base, k, size)
        (wq_own, wq_sib)[k & 1][k >> 1] = wq_scr[pl.ds(at, size), :]


def mid(meta, n_blocks, totals, resids, cotangent, gain, atts, attn_in, group, pieces):
    n, parts, groups = len(pieces), len(resids), len(atts)
    n_totals = len(totals)
    rows, full = cotangent.shape
    width = group[0].shape[1]
    count = rows // CHUNK
    half = n_blocks // 2
    wo = jax.ShapeDtypeStruct((half, full // n_blocks, width), BF16)
    wq = jax.ShapeDtypeStruct((half, full // n_blocks, 3 * width), BF16)
    return pl.pallas_call(
        functools.partial(mid_kernel, n, groups, n_totals, parts, n_blocks),
        out_shape=(
            jax.ShapeDtypeStruct((rows, full), F32),
            jax.ShapeDtypeStruct((rows, full), BF16),
            jax.ShapeDtypeStruct((1, full), F32),
            jax.ShapeDtypeStruct((rows, 3 * width), BF16),
            wo,
            wo,
            wq,
            wq,
        ),
        in_specs=[SMEM] + [VMEM] * (n_totals + parts + 2 + groups + 5) + [ANY] * n,
        out_specs=(VMEM,) * 8,
        scratch_shapes=[
            pltpu.VMEM((width, full), BF16),
            pltpu.VMEM((count, width // PAIR, 2, PAIR, 2 * PAIR), BF16),
            pltpu.VMEM((full, width), BF16),
            pltpu.VMEM((full, 3 * width), BF16),
            pltpu.SemaphoreType.DMA((max(1, width * n // full),)),
        ],
        compiler_params=pltpu.CompilerParams(vmem_limit_bytes=VMEM_LIMIT),
        cost_estimate=pl.CostEstimate(
            flops=8 * 1024 * 1024 * 1024, bytes_accessed=30 * 1024 * 1024, transcendentals=0
        ),
        name="mid",
    )(meta, *totals, *resids, cotangent, gain, *atts, attn_in, *group, *pieces)


def attn_bwd_kernel(n_pieces, position, groups, meta, gmix, fq, fk, val, att, rden, *refs):
    pieces = refs[:n_pieces]
    gproj, w_o, state_scr, sems = refs[n_pieces:]
    width = fq.shape[1]
    group = lax.rem(meta[1] + position, groups)
    for copy in start_group_rows(meta, group, width, pieces, w_o, sems):
        copy.wait()
    attn_bwd_group(fq.shape[0], width, w_o, gmix, fq, fk, val, att, rden, gproj, state_scr)


def attn_bwd(meta, position, groups, gmix, fq, fk, val, att, rden, pieces):
    n = len(pieces)
    rows, full = gmix.shape
    width = fq.shape[1]
    return pl.pallas_call(
        functools.partial(attn_bwd_kernel, n, position, groups),
        out_shape=jax.ShapeDtypeStruct((rows, 3 * width), BF16),
        in_specs=[SMEM] + [VMEM] * 6 + [ANY] * n,
        out_specs=VMEM,
        scratch_shapes=[
            pltpu.VMEM((width, full), BF16),
            pltpu.VMEM((rows // CHUNK, width // PAIR, 2, PAIR, 2 * PAIR), BF16),
            pltpu.SemaphoreType.DMA((max(1, width * n // full),)),
        ],
        compiler_params=pltpu.CompilerParams(vmem_limit_bytes=VMEM_LIMIT),
        cost_estimate=pl.CostEstimate(
            flops=6 * 1024 * 1024 * 1024, bytes_accessed=6 * 1024 * 1024, transcendentals=0
        ),
        name="attn_bwd",
    )(meta, gmix, fq, fk, val, att, rden, *pieces)


def last_kernel(n_pieces, groups, meta, *refs):
    gprojs = refs[:groups]
    tok, gres, gain = refs[groups : groups + 3]
    pieces = refs[groups + 3 : groups + 3 + groups * n_pieces]
    gtok_out, gain_out, weight, sems = refs[groups + 3 + groups * n_pieces :]

    def copies(start):
        found = []
        for j in range(groups):
            mine = pieces[j * n_pieces : (j + 1) * n_pieces]
            size = weight.shape[1] // n_pieces
            for k, piece in enumerate(mine):
                at = pl.multiple_of((meta[0] ^ k) * size, size) if n_pieces > 1 else 0
                found.append(
                    pltpu.make_async_copy(
                        piece, weight.at[j, pl.ds(at, size)], sems.at[j, k]
                    )
                )
        for copy in found:
            if start:
                copy.start()
            else:
                copy.wait()

    @pl.when(pl.program_id(0) == 0)
    def _():
        copies(True)
        gain_out[...] = jnp.zeros_like(gain_out)
        copies(False)

    grad = None
    for j in range(groups):
        part = nt(gprojs[j][...], weight[j])
        grad = part if grad is None else grad + part
    normed, factor = normalize(tok[...].astype(F32))
    gain_out[...] += jnp.sum(grad * normed, 0, keepdims=True)
    gtok_out[...] = gres[...] + norm_back(grad * gain[...], normed, factor)


def last(meta, gprojs, tokens, gres, gain, pieces):
    groups, n = len(pieces), len(pieces[0])
    rows, full = tokens.shape
    flat = [piece for group in pieces for piece in group]

    def rowed(arr):
        return pl.BlockSpec((CHUNK, arr.shape[1]), lambda i: (i, 0))

    return pl.pallas_call(
        functools.partial(last_kernel, n, groups),
        grid=(rows // CHUNK,),
        out_shape=(
            jax.ShapeDtypeStruct((rows, full), F32),
            jax.ShapeDtypeStruct((1, full), F32),
        ),
        in_specs=[SMEM]
        + [rowed(g) for g in gprojs]
        + [rowed(tokens), rowed(gres), pl.BlockSpec(gain.shape, lambda i: (0, 0))]
        + [ANY] * len(flat),
        out_specs=(rowed(gres), pl.BlockSpec((1, full), lambda i: (0, 0))),
        scratch_shapes=[
            pltpu.VMEM((groups, full, flat[0].shape[1]), BF16),
            pltpu.SemaphoreType.DMA((groups, n)),
        ],
        compiler_params=pltpu.CompilerParams(vmem_limit_bytes=VMEM_LIMIT),
        cost_estimate=pl.CostEstimate(
            flops=6 * 1024 * 1024 * 1024, bytes_accessed=20 * 1024 * 1024, transcendentals=0
        ),
        name="last",
    )(meta, *gprojs, tokens, gres, gain, *flat)


def swap(arr, bits, count):
    return lax.ppermute(arr, "dp", [(i, i ^ bits) for i in range(count)])


def gather_pieces(arr, count):
    one = swap(arr, 1, count)
    pieces = [arr, one]
    for bits in range(2, count, 2):
        piece = swap(arr, bits, count)
        pieces += [piece, swap(piece, 1, count)]
    return pieces


def scatter_sum(own, sib, count):
    got = swap(sib, 1, count)
    both = own.astype(F32) + got.astype(F32)
    total = both[0]
    for k in range(1, count // 2):
        total = total + swap(both[k].astype(BF16), 2 * k, count).astype(F32)
    return total


def line_sum(part, index, count):
    if count != 4:
        return lax.psum(part.astype(F32), "mp").astype(BF16)
    inner = (index == 1) | (index == 2)
    got = lax.ppermute(part, "mp", [(0, 1), (3, 2)])
    pair = (part.astype(F32) + got.astype(F32)).astype(BF16)
    other = lax.ppermute(pair, "mp", [(1, 2), (2, 1)])
    total = (pair.astype(F32) + other.astype(F32)).astype(BF16)
    back = lax.ppermute(total, "mp", [(1, 0), (2, 3)])
    return jnp.where(inner, total, back)


def per_device(
    n_dp, n_mp, tokens, lengths, w_qkv, w_out, ln1_gain, ln2_gain, w_in, b_in, w_back, b_back,
    cotangent,
):
    rows, full = tokens.shape
    groups = n_mp
    width = full // groups
    index = lax.axis_index("dp").astype(jnp.int32)
    place = lax.axis_index("mp").astype(jnp.int32)
    paired = n_dp == PAIRED
    base = index if paired else jnp.zeros_like(index)
    meta = jnp.stack([base, place, lengths[0]])

    vectors = lax.all_gather(jnp.stack([ln1_gain, ln2_gain, b_in, b_back]) if ln1_gain.shape == b_in.shape else ln1_gain, "dp", axis=1, tiled=True) if ln1_gain.shape == b_in.shape else None
    if vectors is None:
        gain_one, gain_two, bias_in, bias_back = (
            lax.all_gather(v, "dp", axis=0, tiled=True)[None]
            for v in (ln1_gain, ln2_gain, b_in, b_back)
        )
    else:
        gain_one, gain_two, bias_in, bias_back = (vectors[a][None] for a in range(4))

    def pieces_of(arr, axis):
        if paired:
            return gather_pieces(arr, n_dp)
        return [lax.all_gather(arr, "dp", axis=axis, tiled=True)]

    qkv_parts = w_qkv.astype(BF16).reshape(w_qkv.shape[0], 3, groups, width)
    qkv_pieces = []
    for j in range(groups):
        part = lax.dynamic_index_in_dim(qkv_parts, (place + j) % groups, 2, False)
        qkv_pieces.append(pieces_of(part.reshape(-1, 3 * width), 0))
    out_pieces = pieces_of(w_out.astype(BF16), 0)
    in_pieces = pieces_of(w_in.astype(BF16), 0)
    back_pieces = pieces_of(w_back.astype(BF16), 1)

    normed_one, _ = normalize(tokens.astype(F32))
    attn_in = (normed_one * gain_one).astype(BF16)

    heads = [attn_fwd(meta, attn_in, pieces) for pieces in qkv_pieces]
    atts = [h[3] for h in heads]

    parts = 2
    part_rows = rows // parts
    pieces_mlp = [None] * parts
    for r in reversed(range(parts)):
        pieces_mlp[r] = mlp(
            meta, r * part_rows, part_rows, atts, tokens, cotangent, gain_two, bias_in,
            out_pieces, in_pieces, back_pieces,
        )
    gn_parts, hiddens, gpres, mins, resids = (list(x) for x in zip(*pieces_mlp))

    def chunks_sum(arrs):
        found = [None] * (parts * 2)
        for r in reversed(range(parts)):
            for h in reversed(range(2)):
                size = part_rows // 2
                found[2 * r + h] = line_sum(arrs[r][h * size : (h + 1) * size], place, n_mp)
        return found

    totals = chunks_sum(gn_parts)
    outs = mlp_out(meta, hiddens, back_pieces)
    n_blocks = n_dp
    down_own, down_sib, up_own, up_sib, g_bin, g_bback = mlp_grads(
        meta, n_blocks, hiddens, gpres, mins, cotangent
    )
    out_totals = chunks_sum(outs)
    gres, gmix, g_gain2, gproj0, wo_own, wo_sib, wq_own, wq_sib = mid(
        meta, n_blocks, totals, resids, cotangent, gain_two, atts, attn_in,
        (heads[0][0], heads[0][1], heads[0][2], heads[0][4]), out_pieces,
    )
    gprojs = [gproj0] + [
        attn_bwd(meta, j, groups, gmix, h[0], h[1], h[2], h[3], h[4], out_pieces)
        for j, h in list(enumerate(heads))[1:]
    ]
    grad_tokens, g_gain1 = last(meta, gprojs, tokens, gres, gain_one, qkv_pieces)

    def summed(own, sib):
        if paired:
            return scatter_sum(own, sib, n_dp)
        both = jnp.stack([own, sib], 1).reshape((n_dp,) + own.shape[1:])
        return lax.psum_scatter(both.astype(F32), "dp", scatter_dimension=0)

    grad_back = summed(down_own, down_sib)
    grad_in = summed(up_own, up_sib)
    wo = lax.all_gather(summed(wo_own, wo_sib).astype(BF16), "mp")
    grad_out = jnp.moveaxis(wo, 0, 1).reshape(w_out.shape).astype(F32)
    wq = lax.all_gather(summed(wq_own, wq_sib).astype(BF16), "mp")
    wq = wq.reshape(groups, -1, 3, width)
    grad_qkv = jnp.transpose(wq, (1, 2, 0, 3)).reshape(w_qkv.shape).astype(F32)

    grad_gain1, grad_gain2, grad_bin, grad_bback = (
        lax.psum_scatter(v[0], "dp", scatter_dimension=0, tiled=True)
        for v in (g_gain1, g_gain2, g_bin, g_bback)
    )

    keep = (jnp.arange(rows, dtype=jnp.int32) < lengths[0]).astype(F32)[:, None]
    summed_out = jnp.concatenate(out_totals, 0).astype(F32)
    resid = jnp.concatenate(resids, 0)
    output = ((resid + (summed_out + bias_back)) * keep).astype(BF16)
    return (
        output, grad_tokens, grad_qkv, grad_out, grad_gain1, grad_gain2, grad_in, grad_bin,
        grad_back, grad_bback,
    )


def solution(mesh):
    in_specs = (
        P("dp", None),
        P("dp"),
        P("dp", None),
        P("dp", None),
        P("dp"),
        P("dp"),
        P("dp", "mp"),
        P(("mp", "dp")),
        P("mp", "dp"),
        P("dp"),
        P("dp", None),
    )
    out_specs = (
        P("dp", None),
        P("dp", None),
        P("dp", None),
        P("dp", None),
        P("dp"),
        P("dp"),
        P("dp", "mp"),
        P(("mp", "dp")),
        P("mp", "dp"),
        P("dp"),
    )
    body = functools.partial(per_device, mesh.shape["dp"], mesh.shape["mp"])
    return jax.shard_map(
        body, mesh=mesh, in_specs=in_specs, out_specs=out_specs, check_vma=False
    )
```

```python
import functools

import jax
import jax.numpy as jnp
from jax import lax
from jax.experimental import pallas as pl
from jax.experimental.pallas import tpu as pltpu
from jax.sharding import PartitionSpec as P

HD = 64
PAIR = 2 * HD
CHUNK = 256
EPS = 1e-05
PAIRED = 8
F32 = jnp.float32
BF16 = jnp.bfloat16
VMEM_LIMIT = 16 * 1024 * 1024
GELU_A = 0.7978845608028654
GELU_B = 0.044715


def cost(gflop, mbytes):
    return pl.CostEstimate(
        flops=int(gflop * 1e9), bytes_accessed=int(mbytes * 1e6), transcendentals=0
    )


ANY = pl.BlockSpec(memory_space=pl.ANY)
SMEM = pl.BlockSpec(memory_space=pltpu.SMEM)
VMEM = pl.BlockSpec(memory_space=pltpu.VMEM)


def nn(left, right):
    return jnp.dot(left, right, preferred_element_type=F32)


def nt(left, right):
    return lax.dot_general(left, right, (((1,), (1,)), ((), ())), preferred_element_type=F32)


def tn(left, right):
    return lax.dot_general(left, right, (((0,), (0,)), ((), ())), preferred_element_type=F32)


def normalize(values):
    centre = jnp.mean(values, -1, keepdims=True)
    centred = values - centre
    spread = jnp.mean(centred * centred, -1, keepdims=True)
    factor = lax.rsqrt(spread + EPS)
    return centred * factor, factor


def norm_back(grad, normed, factor):
    return factor * (
        grad
        - jnp.mean(grad, -1, keepdims=True)
        - normed * jnp.mean(grad * normed, -1, keepdims=True)
    )


def owner_of(base, k):
    near = 2 + 2 * (base & 1)
    chip = (0, near, 6 - near, 6)[k >> 1]
    return base ^ (chip if k & 1 == 0 else ((0, 6 - near, near, 6)[k >> 1] ^ 1))


def piece_copies(base, pieces, dst, sems, place=None, cols=None):
    copies = []
    size = dst.shape[0] // len(pieces)
    for k, piece in enumerate(pieces):
        if len(pieces) == 1:
            at = 0
        else:
            owner = owner_of(base, k)
            at = pl.multiple_of((owner if place is None else place(owner)) * size, size)
        start, width = (0, piece.shape[1]) if cols is None else cols
        copies.append(
            pltpu.make_async_copy(
                piece.at[pl.ds(0, size), pl.ds(start, width)], dst.at[pl.ds(at, size)], sems.at[k]
            )
        )
    return copies


def start_all(copies):
    for copy in copies:
        copy.start()


def wait_all(copies):
    for copy in copies:
        copy.wait()


def keep_of(length, start, rows):
    position = lax.broadcasted_iota(jnp.int32, (rows, 1), 0) + start
    return (position < length).astype(F32)


def lane_masks():
    lane = lax.broadcasted_iota(jnp.int32, (CHUNK, PAIR), 1)
    first = (lane < HD).astype(F32)
    return first.astype(BF16), (1.0 - first).astype(BF16)


def block_mask():
    row = lax.broadcasted_iota(jnp.int32, (PAIR, 2 * PAIR), 0)
    col = lax.broadcasted_iota(jnp.int32, (PAIR, 2 * PAIR), 1)
    return ((row < HD) == (col < PAIR)).astype(F32)


def split(state):
    high = state.astype(BF16)
    return high, (state - high.astype(F32)).astype(BF16)


def pair_of(arr, p):
    return arr[:, p * PAIR : (p + 1) * PAIR]


def prep_first_kernel(groups, per, vec_rows, meta, w_qkv, *refs):
    vectors, out = refs[:-1], refs[-1]
    rows, full = w_qkv.shape[0], w_qkv.shape[1] // 3
    width = full // groups
    for j in range(per):
        group = lax.rem(meta[1] + j, groups)
        for t in range(3):
            cols = pl.ds(pl.multiple_of(t * full + group * width, width), width)
            out[pl.ds(0, rows), pl.ds((3 * j + t) * width, width)] = w_qkv[:, cols].astype(BF16)
    if vec_rows:
        highs, mids, lows = [], [], []
        for vector in vectors:
            value = vector[...]
            high = value.astype(BF16).astype(F32)
            middle = (value - high).astype(BF16).astype(F32)
            highs.append(high)
            mids.append(middle)
            lows.append(value - high - middle)
        row = jnp.concatenate(highs + mids + lows, 1)
        out[pl.ds(rows, vec_rows), :] = jnp.broadcast_to(row, (vec_rows, row.shape[1])).astype(
            BF16
        )


def prep_first(meta, groups, per, vec_rows, w_qkv, vectors):
    rows, full = w_qkv.shape
    return pl.pallas_call(
        functools.partial(prep_first_kernel, groups, per, vec_rows),
        out_shape=jax.ShapeDtypeStruct((rows + vec_rows, per * full // groups), BF16),
        in_specs=[SMEM] + [VMEM] * (1 + len(vectors)),
        out_specs=VMEM,
        compiler_params=pltpu.CompilerParams(vmem_limit_bytes=VMEM_LIMIT),
        cost_estimate=cost(0.001, 3),
        name="prep_first",
    )(meta, w_qkv, *vectors)


def prep_rest_kernel(groups, per, bundles, meta, w_qkv, w_out, w_in, w_back, *outs):
    full = w_qkv.shape[1] // 3
    width = full // groups
    for b in range(bundles):
        for j in range(per):
            group = lax.rem(meta[1] + (b + 1) * per + j, groups)
            for t in range(3):
                cols = pl.ds(pl.multiple_of(t * full + group * width, width), width)
                outs[b][:, pl.ds((3 * j + t) * width, width)] = w_qkv[:, cols].astype(BF16)
    out = outs[bundles]
    hidden = w_in.shape[1]
    out[:, pl.ds(0, full)] = w_out[...].astype(BF16)
    out[:, pl.ds(full, hidden)] = w_in[...].astype(BF16)
    step = min(hidden, 256)
    for s in range(hidden // step):
        out[:, pl.ds(full + hidden + s * step, step)] = jnp.transpose(
            w_back[pl.ds(s * step, step), :]
        ).astype(BF16)


def prep_rest(meta, groups, per, w_qkv, w_out, w_in, w_back):
    rows, full = w_qkv.shape
    bundles = groups // per - 1
    shapes = [jax.ShapeDtypeStruct((rows, per * full // groups), BF16)] * bundles
    shapes.append(jax.ShapeDtypeStruct((rows, full // 3 + 2 * w_in.shape[1]), BF16))
    return pl.pallas_call(
        functools.partial(prep_rest_kernel, groups, per, bundles),
        out_shape=tuple(shapes),
        in_specs=[SMEM] + [VMEM] * 4,
        out_specs=(VMEM,) * len(shapes),
        compiler_params=pltpu.CompilerParams(vmem_limit_bytes=VMEM_LIMIT),
        cost_estimate=cost(0.001, 5),
        name="prep_rest",
    )(meta, w_qkv, w_out, w_in, w_back)


def attn_fwd_kernel(n_pieces, count_vec, start, meta, source, *refs):
    pieces = refs[:n_pieces]
    fq_out, fk_out, val_out, att_out, rden_out = refs[n_pieces : n_pieces + 5]
    rest = refs[n_pieces + 5 :]
    if count_vec:
        attn_in, vec_out, weight, states, sems, vec_scr, vec_sems = rest
    else:
        weight, states, sems = rest
        attn_in = source
    width = fq_out.shape[1]
    pairs = width // PAIR

    @pl.when(pl.program_id(0) == 0)
    def _():
        copies = piece_copies(meta[0], pieces, weight, sems, None, (start, 3 * width))
        moves = []
        if count_vec:
            size = vec_out.shape[1] // n_pieces
            moves = [
                pltpu.make_async_copy(
                    piece.at[pl.ds(size, vec_scr.shape[1])], vec_scr.at[k], vec_sems.at[k]
                )
                for k, piece in enumerate(pieces)
            ]
        start_all(moves + copies)
        for k, move in enumerate(moves):
            move.wait()
            value = vec_scr[k].astype(F32)[0:1]
            at = pl.ds(pl.multiple_of(owner_of(meta[0], k) * size, size), size)
            for a in range(count_vec):
                parts = [
                    value[:, (t * count_vec + a) * size : (t * count_vec + a + 1) * size]
                    for t in range(3)
                ]
                vec_out[a : a + 1, at] = parts[0] + parts[1] + parts[2]
        states[...] = jnp.zeros_like(states)
        wait_all(copies)

    if count_vec:
        attn_in[...] = (source[...] * vec_out[0:1, :]).astype(BF16)
    mask_a, mask_b = lane_masks()
    blocks = block_mask()
    first = lax.broadcasted_iota(jnp.int32, (CHUNK, PAIR), 1) < HD
    causal = lax.broadcasted_iota(jnp.int32, (CHUNK, CHUNK), 0) >= lax.broadcasted_iota(
        jnp.int32, (CHUNK, CHUNK), 1
    )
    proj = nn(attn_in[...], weight[...])
    query, keys = proj[:, :width], proj[:, width : 2 * width]
    fq = jnp.where(query > 0, query + 1.0, jnp.exp(jnp.minimum(query, 0.0))).astype(BF16)
    fk = jnp.where(keys > 0, keys + 1.0, jnp.exp(jnp.minimum(keys, 0.0))).astype(BF16)
    val = proj[:, 2 * width :].astype(BF16)
    fq_out[...] = fq
    fk_out[...] = fk
    val_out[...] = val
    for p in range(pairs):
        q, k, v = pair_of(fq, p), pair_of(fk, p), pair_of(val, p)
        v_a = v * mask_a + mask_b
        v_b = v * mask_b + mask_a
        s_a = jnp.where(causal, nt(q * mask_a, k), 0.0).astype(BF16)
        s_b = jnp.where(causal, nt(q * mask_b, k), 0.0).astype(BF16)
        high, low = split(states[p])
        past = nn(q, high) + nn(q, low)
        r_a = nn(s_a, v_a) + past[:, :PAIR]
        r_b = nn(s_b, v_b) + past[:, PAIR:]
        numer = jnp.where(first, r_a, r_b)
        denom = pltpu.roll(jnp.where(first, r_b, r_a), HD, axis=1)
        inverse = 1.0 / denom
        cols = pl.ds(p * PAIR, PAIR)
        att_out[:, cols] = (numer * inverse).astype(BF16)
        rden_out[:, cols] = inverse
        states[p] = states[p] + tn(k, jnp.concatenate([v_a, v_b], 1)) * blocks


def attn_fwd(meta, source, pieces, groups, position, count_vec):
    rows, full = source.shape
    width = full // groups
    n = len(pieces)
    low = jax.ShapeDtypeStruct((rows, width), BF16)
    shapes = [low, low, low, low, jax.ShapeDtypeStruct((rows, width), F32)]
    specs = [pl.BlockSpec((CHUNK, width), lambda i: (i, 0))] * 5
    wide = pl.BlockSpec((CHUNK, full), lambda i: (i, 0))
    scratch = [
        pltpu.VMEM((full, 3 * width), BF16),
        pltpu.VMEM((width // PAIR, PAIR, 2 * PAIR), F32),
        pltpu.SemaphoreType.DMA((n,)),
    ]
    if count_vec:
        shapes += [
            jax.ShapeDtypeStruct((rows, full), BF16),
            jax.ShapeDtypeStruct((count_vec, full), F32),
        ]
        specs += [wide, pl.BlockSpec((count_vec, full), lambda i: (0, 0))]
        vec_rows = pieces[0].shape[0] - full // n
        scratch += [
            pltpu.VMEM((n, vec_rows, pieces[0].shape[1]), BF16),
            pltpu.SemaphoreType.DMA((n,)),
        ]
    return pl.pallas_call(
        functools.partial(attn_fwd_kernel, n, count_vec, position * 3 * width),
        grid=(rows // CHUNK,),
        out_shape=tuple(shapes),
        in_specs=[SMEM, wide] + [ANY] * n,
        out_specs=tuple(specs),
        scratch_shapes=scratch,
        compiler_params=pltpu.CompilerParams(vmem_limit_bytes=VMEM_LIMIT),
        cost_estimate=cost(8, 6),
        name="attn_fwd",
    )(meta, source, *pieces)


def rest_copies(meta, which, pieces, dst, sems, groups):
    n = len(pieces)
    full = dst.shape[0]
    if which:
        hidden = dst.shape[1]
        cols = (full + (which - 1) * hidden, hidden)
        return piece_copies(meta[0], pieces, dst, sems.at[which], None, cols)
    width = full // groups
    if n == 1:
        found = []
        for j in range(groups):
            at = pl.multiple_of(lax.rem(meta[1] + j, groups) * width, width)
            found.append(
                pltpu.make_async_copy(
                    pieces[0].at[pl.ds(at, width), pl.ds(0, full)],
                    dst.at[pl.ds(j * width, width)],
                    sems.at[0, j],
                )
            )
        return found
    span = n // groups

    def turned(owner):
        group = lax.rem(owner // span - meta[1] + groups, groups)
        return group * span + lax.rem(owner, span)

    return piece_copies(meta[0], pieces, dst, sems.at[0], turned, (0, full))


def mlp_kernel(n_pieces, n_atts, groups, part, meta, *refs):
    atts = refs[:n_atts]
    tok, cot, vec, bias = refs[n_atts : n_atts + 4]
    pieces = refs[n_atts + 4 : n_atts + 4 + n_pieces]
    refs = refs[n_atts + 4 + n_pieces :]
    send_out, keep_out, hidden_out, gpre_out, min_out, resid_out = refs[:6]
    w_o, w_i, w_b, sems = refs[6:]
    i = pl.program_id(0)

    def loads(which):
        return rest_copies(meta, which, pieces, (w_o, w_i, w_b)[which], sems, groups)

    @pl.when(i == 0)
    def _():
        for which in range(3):
            start_all(loads(which))
        wait_all(loads(0))

    gain = vec[1:2, :]
    start = (2 * part + (i ^ (1 - meta[3]))) * CHUNK
    keep = keep_of(meta[2], start, CHUNK)
    g_low = (cot[...].astype(F32) * keep).astype(BF16)
    mixed = nn(jnp.concatenate([att[...] for att in atts], 1), w_o[...])
    resid = tok[...].astype(F32) + mixed
    resid_out[...] = resid
    normed, _ = normalize(resid)
    mlp_in = (normed * gain).astype(BF16)
    min_out[...] = mlp_in

    @pl.when(i == 0)
    def _():
        wait_all(loads(1))
        wait_all(loads(2))

    pre = nn(mlp_in, w_i[...]) + bias[...]
    square = pre * pre
    t = jnp.tanh(GELU_A * pre * (1.0 + GELU_B * square))
    half = 0.5 * (1.0 + t)
    hidden_out[...] = (pre * half).astype(BF16)
    slope = half + (0.5 * GELU_A) * pre * (1.0 - t * t) * (1.0 + (3.0 * GELU_B) * square)
    gpre = (nn(g_low, w_b[...]) * slope).astype(BF16)
    gpre_out[...] = gpre
    grad = nt(gpre, w_i[...]).astype(BF16)

    @pl.when(i == 0)
    def _():
        send_out[...] = grad

    @pl.when(i == 1)
    def _():
        keep_out[...] = grad


def mlp(meta, part, atts, groups, tokens, cotangent, vec, bias, pieces):
    n, n_atts = len(pieces), len(atts)
    rows = 2 * CHUNK
    width, hidden = tokens.shape[1], bias.shape[1]

    def rowed(cols, base):
        return pl.BlockSpec((CHUNK, cols), lambda i, m: (base + (i ^ (1 - m[3])), 0))

    def whole(shape):
        return pl.BlockSpec(shape, lambda i, m: (0, 0))

    shapes = [(CHUNK, width), (CHUNK, width), (rows, hidden), (rows, hidden), (rows, width)]
    return pl.pallas_call(
        functools.partial(mlp_kernel, n, n_atts, groups, part),
        out_shape=tuple(jax.ShapeDtypeStruct(shape, BF16) for shape in shapes)
        + (jax.ShapeDtypeStruct((rows, width), F32),),
        grid_spec=pltpu.PrefetchScalarGridSpec(
            num_scalar_prefetch=1,
            grid=(2,),
            in_specs=[rowed(a.shape[1], 2 * part) for a in atts]
            + [rowed(width, 2 * part)] * 2
            + [whole(vec.shape), whole(bias.shape)]
            + [ANY] * n,
            out_specs=(
                whole((CHUNK, width)),
                whole((CHUNK, width)),
                rowed(hidden, 0),
                rowed(hidden, 0),
                rowed(width, 0),
                rowed(width, 0),
            ),
            scratch_shapes=[
                pltpu.VMEM((width, width), BF16),
                pltpu.VMEM((width, hidden), BF16),
                pltpu.VMEM((width, hidden), BF16),
                pltpu.SemaphoreType.DMA((3, max(n, groups))),
            ],
        ),
        compiler_params=pltpu.CompilerParams(vmem_limit_bytes=VMEM_LIMIT),
        cost_estimate=cost(8, 16),
        name="mlp_fwd_bwd",
    )(meta, *atts, tokens, cotangent, vec, bias, *pieces)


def mlp_out_kernel(n_pieces, parts, meta, *refs):
    hiddens = refs[:parts]
    pieces = refs[parts : parts + n_pieces]
    send, keep, w_b, sems = refs[parts + n_pieces :]
    copies = rest_copies(meta, 2, pieces, w_b, sems, 1)
    start_all(copies)
    wait_all(copies)
    for c, out in enumerate((send, keep)):
        at = pl.multiple_of((c ^ (1 - meta[3])) * CHUNK, CHUNK)
        for r in range(parts):
            out[pl.ds(r * CHUNK, CHUNK), :] = nt(hiddens[r][pl.ds(at, CHUNK), :], w_b[...]).astype(
                BF16
            )


def mlp_out(meta, hiddens, pieces, width):
    n, parts = len(pieces), len(hiddens)
    hidden = hiddens[0].shape[1]
    return pl.pallas_call(
        functools.partial(mlp_out_kernel, n, parts),
        out_shape=(jax.ShapeDtypeStruct((parts * CHUNK, width), BF16),) * 2,
        in_specs=[SMEM] + [VMEM] * parts + [ANY] * n,
        out_specs=(VMEM,) * 2,
        scratch_shapes=[
            pltpu.VMEM((width, hidden), BF16),
            pltpu.SemaphoreType.DMA((3, n)),
        ],
        compiler_params=pltpu.CompilerParams(vmem_limit_bytes=VMEM_LIMIT),
        cost_estimate=cost(4, 8),
        name="mlp_out",
    )(meta, *hiddens, *pieces)


def offset_of(n_blocks, base, k, size):
    return pl.multiple_of((base ^ k) * size, size) if n_blocks == PAIRED else k * size


def spread(n_blocks, base, scratch, own, sib, start):
    size = own.shape[1]
    cols = pl.ds(start, scratch.shape[1])
    for k in range(n_blocks):
        at = offset_of(n_blocks, base, k, size)
        (own, sib)[k & 1][k >> 1, :, cols] = scratch[pl.ds(at, size), :]


def mlp_grads_kernel(n_blocks, parts, meta, *refs):
    hiddens, gpres, mins = (refs[a * parts : (a + 1) * parts] for a in range(3))
    cot = refs[3 * parts]
    own, sib, bin_out, bback_out, scratch, g_low = refs[3 * parts + 1 :]
    rows = hiddens[0].shape[0]
    total_in = total_back = None
    for r in range(parts):
        keep = keep_of(meta[2], r * rows, rows)
        g = cot[pl.ds(r * rows, rows), :].astype(F32) * keep
        g_low[pl.ds(r * rows, rows), :] = g.astype(BF16)
        back = jnp.sum(g, 0, keepdims=True)
        inner = jnp.sum(gpres[r][...].astype(F32), 0, keepdims=True)
        total_in = inner if total_in is None else total_in + inner
        total_back = back if total_back is None else total_back + back
    bin_out[...] = total_in
    bback_out[...] = total_back
    step = 256
    hidden = hiddens[0].shape[1]
    for s in range(scratch.shape[0] // step):
        cols = pl.ds(s * step, step)
        up = down = None
        for r in range(parts):
            part = tn(mins[r][:, cols], gpres[r][...])
            up = part if up is None else up + part
            part = tn(g_low[pl.ds(r * rows, rows), cols], hiddens[r][...])
            down = part if down is None else down + part
        scratch[cols, pl.ds(0, hidden)] = up.astype(BF16)
        scratch[cols, pl.ds(hidden, hidden)] = down.astype(BF16)
    spread(n_blocks, meta[0], scratch, own, sib, 0)


def mlp_grads(meta, n_blocks, hiddens, gpres, mins, cotangent):
    parts = len(hiddens)
    hidden, width = hiddens[0].shape[1], mins[0].shape[1]
    blocks = jax.ShapeDtypeStruct((n_blocks // 2, width // n_blocks, 2 * hidden), BF16)
    return pl.pallas_call(
        functools.partial(mlp_grads_kernel, n_blocks, parts),
        out_shape=(
            blocks,
            blocks,
            jax.ShapeDtypeStruct((1, hidden), F32),
            jax.ShapeDtypeStruct((1, width), F32),
        ),
        in_specs=[SMEM] + [VMEM] * (3 * parts + 1),
        out_specs=(VMEM,) * 4,
        scratch_shapes=[
            pltpu.VMEM((width, 2 * hidden), BF16),
            pltpu.VMEM(cotangent.shape, BF16),
        ],
        compiler_params=pltpu.CompilerParams(vmem_limit_bytes=VMEM_LIMIT),
        cost_estimate=cost(8, 16),
        name="mlp_grads",
    )(meta, *hiddens, *gpres, *mins, cotangent)


def norm_bwd_kernel(parts, meta, *refs):
    totals = refs[: 2 * parts]
    resids = refs[2 * parts : 3 * parts]
    cot, vec, gres_out, gmix_out, gain_out = refs[3 * parts :]
    i = pl.program_id(0)
    chunk = 2 * (i // 2) + (lax.rem(i, 2) ^ meta[3])
    keep = keep_of(meta[2], chunk * CHUNK, CHUNK)

    @pl.when(i == 0)
    def _():
        gain_out[...] = jnp.zeros_like(gain_out)

    for r in range(parts):
        for h in range(2):

            @pl.when(i == 2 * r + h)
            def _():
                grad = totals[2 * r + h][...].astype(F32)
                normed, factor = normalize(resids[r][...])
                gain_out[...] += jnp.sum(grad * normed, 0, keepdims=True)
                gres = cot[...].astype(F32) * keep + norm_back(
                    grad * vec[1:2, :], normed, factor
                )
                gres_out[...] = gres
                gmix_out[...] = gres.astype(BF16)


def norm_bwd(meta, totals, resids, cotangent, vec):
    parts = len(resids)
    rows, full = cotangent.shape

    def whole(shape):
        return pl.BlockSpec(shape, lambda i, m: (0, 0))

    def inner(r):
        def index(i, m):
            bit = lax.rem(jnp.clip(i - 2 * r, 0, 1), 2)
            return (bit ^ m[3], 0)

        return pl.BlockSpec((CHUNK, full), index)

    rowed = pl.BlockSpec((CHUNK, full), lambda i, m: (2 * (i // 2) + (lax.rem(i, 2) ^ m[3]), 0))
    return pl.pallas_call(
        functools.partial(norm_bwd_kernel, parts),
        out_shape=(
            jax.ShapeDtypeStruct((rows, full), F32),
            jax.ShapeDtypeStruct((rows, full), BF16),
            jax.ShapeDtypeStruct((1, full), F32),
        ),
        grid_spec=pltpu.PrefetchScalarGridSpec(
            num_scalar_prefetch=1,
            grid=(2 * parts,),
            in_specs=[whole(t.shape) for t in totals]
            + [inner(r) for r in range(parts)]
            + [rowed, whole(vec.shape)],
            out_specs=(rowed, rowed, whole((1, full))),
        ),
        compiler_params=pltpu.CompilerParams(vmem_limit_bytes=VMEM_LIMIT),
        cost_estimate=cost(1, 16),
        name="norm_bwd",
    )(meta, *totals, *resids, cotangent, vec)


def group_rows(meta, group, width, pieces, dst, sems, start):
    full = dst.shape[1]
    if len(pieces) == 1:
        at = pl.multiple_of(group * width, width)
        copy = pltpu.make_async_copy(
            pieces[0].at[pl.ds(at, width), pl.ds(0, full)], dst, sems.at[0]
        )
        return copy.start() if start else copy.wait()
    size = pieces[0].shape[0]
    for part in range(width // size):
        wanted = group * (width // size) + part
        target = dst.at[pl.ds(part * size, size)]
        if not start:
            pltpu.make_async_copy(
                pieces[0].at[:, pl.ds(0, full)], target, sems.at[part]
            ).wait()
            continue
        for k, piece in enumerate(pieces):

            @pl.when(wanted == owner_of(meta[0], k))
            def _():
                pltpu.make_async_copy(
                    piece.at[:, pl.ds(0, full)], target, sems.at[part]
                ).start()


def attn_bwd_kernel(shape, meta, *refs):
    n, groups, position, start, n_atts, n_vectors, n_blocks = shape
    is_first, is_last = position == 0, position == groups - 1
    refs = list(refs)

    def take(count):
        found = refs[:count]
        del refs[:count]
        return found

    gmix, fq, fk, val, att, rden = take(6)
    (acc_in,) = take(1) if not is_first else (None,)
    attn_in, *atts = take(1 + n_atts) if is_first else (None,)
    tok, gres, vec, *vectors = take(3 + n_vectors) if is_last else (None, None, None)
    pieces_o, pieces_w = take(n), take(n)
    (acc_out,) = take(1)
    own, sib = take(2) if is_first or is_last else (None, None)
    w_o, w_q, state_scr, later, sems_o, sems_w = take(6)
    width = fq.shape[1]
    pairs = width // PAIR
    full = gmix.shape[1]
    i = pl.program_id(0)
    count = fk.shape[0] // CHUNK
    c = count - 1 - i
    place = meta[1]
    group = lax.rem(place + position, groups)
    mask_a, mask_b = lane_masks()
    blocks = block_mask()

    def weight_copies():
        return piece_copies(meta[0], pieces_w, w_q, sems_w, None, (start, 3 * width))

    def side_copies():
        found = [pltpu.make_async_copy(attn_in, ain_scr, side_sems.at[0])]
        for a in range(n_atts):
            found.append(
                pltpu.make_async_copy(
                    atts[a], att_scr.at[:, pl.ds(a * width, width)], side_sems.at[a + 1]
                )
            )
        return found

    if is_first:
        gproj_scr, gcol_scr, ain_scr, att_scr, product, side_sems = take(6)
    if is_last:
        (gain_scr,) = take(1)

    @pl.when(i == 0)
    def _():
        group_rows(meta, group, width, pieces_o, w_o, sems_o, True)
        start_all(weight_copies())
        if is_first:
            start_all(side_copies())
        if is_last:
            gain_scr[...] = jnp.zeros_like(gain_scr)
        later[...] = jnp.zeros_like(later)
        for p in range(pairs):
            state = jnp.zeros((PAIR, 2 * PAIR), F32)
            for s in range(count):
                high, low = split(state)
                state_scr[s, p, 0] = high
                state_scr[s, p, 1] = low
                if s + 1 < count:
                    rows, cols = pl.ds(s * CHUNK, CHUNK), pl.ds(p * PAIR, PAIR)
                    v = val[rows, cols]
                    aug = jnp.concatenate([v * mask_a + mask_b, v * mask_b + mask_a], 1)
                    state = state + tn(fk[rows, cols], aug) * blocks
        group_rows(meta, group, width, pieces_o, w_o, sems_o, False)
        wait_all(weight_copies())

    first = lax.broadcasted_iota(jnp.int32, (CHUNK, PAIR), 1) < HD
    row = lax.broadcasted_iota(jnp.int32, (CHUNK, CHUNK), 0)
    col = lax.broadcasted_iota(jnp.int32, (CHUNK, CHUNK), 1)
    causal, causal_t = row >= col, row <= col
    head_row = lax.broadcasted_iota(jnp.int32, (width, width), 0) // HD
    head_col = lax.broadcasted_iota(jnp.int32, (width, width), 1) // HD
    head_sum = (head_row == head_col).astype(F32).astype(BF16)
    rows = pl.ds(pl.multiple_of(c * CHUNK, CHUNK), CHUNK)
    grad_att = nt(gmix[...], w_o[...])
    inverse = rden[...]
    gnum = (grad_att * inverse).astype(BF16)
    dots = nn((grad_att * att[...].astype(F32)).astype(BF16), head_sum)
    gden = (-dots * inverse).astype(BF16).astype(F32)
    found_q, found_k, found_v = [], [], []
    for p in range(pairs):
        cols = pl.ds(p * PAIR, PAIR)
        q, k, v = fq[:, cols], fk[rows, cols], val[rows, cols]
        num = pair_of(gnum, p)
        den = (pltpu.roll(pair_of(gden, p), HD, axis=1) * (1.0 / HD)).astype(BF16)
        n_a, n_b = num * mask_a + den * mask_b, num * mask_b + den * mask_a
        q_a, q_b = q * mask_a, q * mask_b
        v_a, v_b = v * mask_a + mask_b, v * mask_b + mask_a
        n_cat = jnp.concatenate([n_a, n_b], 1)
        v_cat = jnp.concatenate([v_a, v_b], 1)
        st_a = jnp.where(causal_t, nt(k, q_a), 0.0).astype(BF16)
        st_b = jnp.where(causal_t, nt(k, q_b), 0.0).astype(BF16)
        gs_a = jnp.where(causal, nt(n_a, v_a), 0.0).astype(BF16)
        gs_b = jnp.where(causal, nt(n_b, v_b), 0.0).astype(BF16)
        gt_a = jnp.where(causal_t, nt(v_a, n_a), 0.0).astype(BF16)
        gt_b = jnp.where(causal_t, nt(v_b, n_b), 0.0).astype(BF16)
        high, low = split(later[p])
        past = nn(k, high) + nn(k, low)
        gq = nn(gs_a, k * mask_a) + nn(gs_b, k * mask_b)
        gq = gq + nt(n_cat, state_scr[c, p, 0]) + nt(n_cat, state_scr[c, p, 1])
        gk = nn(gt_a, q_a) + nn(gt_b, q_b) + nt(v_cat, high) + nt(v_cat, low)
        gv = nn(st_a, num * mask_a) + nn(st_b, num * mask_b)
        gv = gv + jnp.where(first, past[:, :PAIR], past[:, PAIR:])
        later[p] = later[p] + tn(q, n_cat) * blocks
        found_q.append((gq * jnp.minimum(q.astype(F32), 1.0)).astype(BF16))
        found_k.append((gk * jnp.minimum(k.astype(F32), 1.0)).astype(BF16))
        found_v.append(gv.astype(BF16))
    gproj = jnp.concatenate(found_q + found_k + found_v, 1)
    grad = nt(gproj, w_q[...])
    if not is_first:
        grad = grad + acc_in[...]
    if not is_last:
        acc_out[...] = grad
    else:
        normed, factor = normalize(tok[...].astype(F32))
        gain_scr[...] += jnp.sum(grad * normed, 0, keepdims=True)
        acc_out[...] = gres[...] + norm_back(grad * vec[0:1, :], normed, factor)

        @pl.when(i == count - 1)
        def _():
            for a, source in enumerate([gain_scr] + vectors):
                size = source.shape[1] // n_blocks
                for k in range(n_blocks):
                    at = offset_of(n_blocks, meta[0], k, size)
                    (own, sib)[k & 1][k >> 1, a : a + 1, pl.ds(0, size)] = source[
                        :, pl.ds(at, size)
                    ]

    if is_first:
        gproj_scr[rows, :] = gproj
        gcol_scr[rows, :] = gmix[:, pl.ds(pl.multiple_of(place * width, width), width)]

        @pl.when(i == count - 1)
        def _():
            wait_all(side_copies())
            for s in range(full // 256):
                piece = pl.ds(s * 256, 256)
                product[piece, pl.ds(0, 3 * width)] = tn(
                    ain_scr[:, s * 256 : (s + 1) * 256], gproj_scr[...]
                ).astype(BF16)
            for j in range(groups):
                at = pl.multiple_of(lax.rem(place + j, groups) * width, width)
                product[pl.ds(at, width), pl.ds(3 * width, width)] = tn(
                    att_scr[:, j * width : (j + 1) * width], gcol_scr[...]
                ).astype(BF16)
            spread(n_blocks, meta[0], product, own, sib, 0)


def attn_bwd(meta, n_blocks, position, start, gmix, heads, pieces_o, pieces_w, extra):
    n = len(pieces_o)
    rows, full = gmix.shape
    width = heads[0].shape[1]
    groups = full // width
    count = rows // CHUNK
    is_first, is_last = position == 0, position == groups - 1

    def rowed(cols):
        return pl.BlockSpec((CHUNK, cols), lambda i: (count - 1 - i, 0))

    def whole(shape):
        return pl.BlockSpec(shape, lambda i: (0,) * len(shape))

    specs = [rowed(full), rowed(width), whole((rows, width)), whole((rows, width))]
    specs += [rowed(width), rowed(width)]
    n_atts = n_vectors = 0
    if is_first:
        n_atts = len(extra) - 1
        specs += [ANY] * len(extra)
    else:
        specs += [rowed(full)]
    if is_last:
        n_vectors = len(extra) - 4
        specs += [rowed(full), rowed(full)] + [whole(v.shape) for v in extra[3:]]
    shapes, outs = [jax.ShapeDtypeStruct((rows, full), F32)], [rowed(full)]
    scratch = [
        pltpu.VMEM((width, full), BF16),
        pltpu.VMEM((full, 3 * width), BF16),
        pltpu.VMEM((count, width // PAIR, 2, PAIR, 2 * PAIR), BF16),
        pltpu.VMEM((width // PAIR, PAIR, 2 * PAIR), F32),
        pltpu.SemaphoreType.DMA((max(1, width * n // full),)),
        pltpu.SemaphoreType.DMA((n,)),
    ]
    if is_first:
        blocks = (n_blocks // 2, full // n_blocks, 4 * width)
        shapes += [jax.ShapeDtypeStruct(blocks, BF16)] * 2
        outs += [whole(blocks)] * 2
        scratch += [
            pltpu.VMEM((rows, 3 * width), BF16),
            pltpu.VMEM((rows, width), BF16),
            pltpu.VMEM((rows, full), BF16),
            pltpu.VMEM((rows, full), BF16),
            pltpu.VMEM((full, 4 * width), BF16),
            pltpu.SemaphoreType.DMA((n_atts + 1,)),
        ]
    if is_last:
        small = (n_blocks // 2, 4, full // n_blocks)
        shapes += [jax.ShapeDtypeStruct(small, F32)] * 2
        outs += [whole(small)] * 2
        scratch += [pltpu.VMEM((1, full), F32)]
    shape = (n, groups, position, start, n_atts, n_vectors, n_blocks)
    return pl.pallas_call(
        functools.partial(attn_bwd_kernel, shape),
        grid=(count,),
        out_shape=tuple(shapes),
        in_specs=[SMEM] + specs + [ANY] * (2 * n),
        out_specs=tuple(outs),
        scratch_shapes=scratch,
        compiler_params=pltpu.CompilerParams(vmem_limit_bytes=VMEM_LIMIT),
        cost_estimate=cost(10, 7),
        name="attn_bwd",
    )(meta, gmix, *heads, *extra, *pieces_o, *pieces_w)


def finish_kernel(parts, meta, *refs):
    resids = refs[:parts]
    kept, other, vec, out = refs[parts:]
    bias = vec[3:4, :]
    for r in range(parts):
        for source, h in ((kept, 0), (other, 1)):
            inner = pl.multiple_of((h ^ meta[3]) * CHUNK, CHUNK)
            at = pl.multiple_of(r * 2 * CHUNK + inner, CHUNK)
            summed = source[pl.ds(r * CHUNK, CHUNK), :].astype(F32)
            total = resids[r][pl.ds(inner, CHUNK), :] + (summed + bias)
            keep = keep_of(meta[2], at, CHUNK)
            out[pl.ds(at, CHUNK), :] = (total * keep).astype(BF16)


def finish(meta, resids, kept, other, vec):
    rows, width = 2 * CHUNK * len(resids), kept.shape[1]
    return pl.pallas_call(
        functools.partial(finish_kernel, len(resids)),
        out_shape=jax.ShapeDtypeStruct((rows, width), BF16),
        in_specs=[SMEM] + [VMEM] * (len(resids) + 3),
        out_specs=VMEM,
        compiler_params=pltpu.CompilerParams(vmem_limit_bytes=VMEM_LIMIT),
        cost_estimate=cost(0.01, 8),
        name="finish",
    )(meta, *resids, kept, other, vec)


def assemble_kernel(groups, turned, meta, *refs):
    pieces, (qkv, out) = refs[:-2], refs[-2:]
    width = out.shape[1] // groups
    for d, piece in enumerate(pieces):
        group = lax.rem(meta[1] - d + groups, groups) if turned else d
        for t in range(4):
            value = piece[:, pl.ds(t * width, width)].astype(F32)
            start = t % 3 * groups * width + group * width
            at = pl.ds(pl.multiple_of(start, width), width)
            (out if t == 3 else qkv)[:, at] = value


def assemble(meta, groups, turned, pieces):
    rows, width = pieces[0].shape[0], pieces[0].shape[1] // 4
    return pl.pallas_call(
        functools.partial(assemble_kernel, groups, turned),
        out_shape=(
            jax.ShapeDtypeStruct((rows, 3 * groups * width), F32),
            jax.ShapeDtypeStruct((rows, groups * width), F32),
        ),
        in_specs=[SMEM] + [VMEM] * len(pieces),
        out_specs=(VMEM,) * 2,
        compiler_params=pltpu.CompilerParams(vmem_limit_bytes=VMEM_LIMIT),
        cost_estimate=cost(0.01, 3),
        name="assemble",
    )(meta, *pieces)


def send(arr, move):
    return lax.ppermute(arr, "dp", [(i, move(i)) for i in range(PAIRED)])


def near(i):
    return i ^ (4 if i & 1 else 2)


def far(i):
    return i ^ (2 if i & 1 else 4)


def across(i):
    return i ^ 1


def after(arrs, *deps):
    return lax.optimization_barrier((arrs, deps))[0]


def gather_pieces(arr):
    one, two = send(arr, near), send(arr, far)
    three = send(one, far)
    pieces = []
    for piece in (arr, one, two, three):
        pieces += [piece, send(piece, across)]
    return pieces


def chip_sum(own, sib):
    return own.astype(F32) + send(sib, across).astype(F32)


def plane_sum(both, kind):
    total = both[0]
    for k in range(1, PAIRED // 2):
        moved = send(both[k].astype(kind), lambda i, k=k: i ^ (2 * k))
        total = total + moved.astype(F32)
    return total


def swapped(arr, bits):
    return lax.ppermute(arr, "mp", [(i, i ^ bits) for i in range(4)])


def add_low(left, right):
    return (left.astype(F32) + right.astype(F32)).astype(BF16)


def per_device(
    n_dp, n_mp, tokens, lengths, w_qkv, w_out, ln1_gain, ln2_gain, w_in, b_in, w_back, b_back,
    cotangent,
):
    rows, full = tokens.shape
    groups = n_mp
    per = 2
    paired = n_dp == PAIRED and n_mp == 4
    index = lax.axis_index("dp").astype(jnp.int32)
    place = lax.axis_index("mp").astype(jnp.int32)
    zero = jnp.zeros_like(index)
    meta = jnp.stack(
        [index if paired else zero, place, lengths[0], (place & 1) if paired else zero]
    )
    vectors = [v[None] for v in (ln1_gain, ln2_gain, b_in, b_back)]

    def gather(arr, axis=0):
        return lax.all_gather(arr, "dp", axis=axis, tiled=True)

    first_sent = prep_first(
        meta, groups, per, 16 if paired else 0, w_qkv, vectors if paired else ()
    )
    normed_one, _ = normalize(tokens.astype(F32))
    parts = rows // (2 * CHUNK)
    found, totals = [None] * parts, [None] * (2 * parts)

    if not paired:
        sent = [first_sent] + list(prep_rest(meta, groups, per, w_qkv, w_out, w_in, w_back))
        gathered = [[gather(arr)] for arr in sent]
        bundles, rest = gathered[:-1], gathered[-1]
        gain_one, gain_two, bias, bias_back = (gather(v, 1) for v in vectors)
        attn_in = (normed_one * gain_one).astype(BF16)
        vec = jnp.concatenate([gain_one, gain_two, gain_two, bias_back], 0)
        heads = [
            attn_fwd(meta, attn_in, bundles[j // per], groups, j % per, 0) for j in range(groups)
        ]
    else:
        bundles = [gather_pieces(first_sent)]
        raw = after((w_qkv, w_out, w_in, w_back), bundles[0][1])
        second, third = prep_rest(meta, groups, per, *raw)
        bundles.append(gather_pieces(second))
        rest = gather_pieces(after(third, bundles[0][2]))
        heads = [attn_fwd(meta, after(normed_one, bundles[1][2]), bundles[0], groups, 0, 4)]
        attn_in, vec = heads[0][5:]
        bias = vec[2:3]
        heads.append(attn_fwd(meta, attn_in, bundles[0], groups, 1, 0))
        attn_in = after(attn_in, rest[2])
        heads.append(attn_fwd(meta, attn_in, bundles[1], groups, 0, 0))
        heads.append(attn_fwd(meta, attn_in, bundles[1], groups, 1, 0))
    heads = [h[:5] for h in heads]
    atts = [h[3] for h in heads]

    for r in reversed(range(parts)):
        found[r] = mlp(meta, r, atts, groups, tokens, cotangent, vec, bias, rest)
    aways, keeps, hiddens, gpres, mins, resids = (list(x) for x in zip(*found))
    if paired:
        pairs = [None] * parts
        for r in reversed(range(parts)):
            pairs[r] = add_low(keeps[r], swapped(aways[r], 1))
        for r in reversed(range(parts)):
            totals[2 * r] = add_low(pairs[r], swapped(pairs[r], 2))
            totals[2 * r + 1] = swapped(totals[2 * r], 1)
    own, sib, g_bin, g_bback = mlp_grads(meta, n_dp, hiddens, gpres, mins, cotangent)
    out_away, out_kept = mlp_out(meta, hiddens, rest, full)

    def stacked_sum(own, sib):
        both = jnp.stack([own, sib], 1).reshape((n_dp,) + own.shape[1:])
        return lax.psum_scatter(both.astype(F32), "dp", scatter_dimension=0)

    def mp_sum(arr):
        return lax.psum(arr.astype(F32), "mp").astype(BF16)

    if not paired:
        for r in range(parts):
            totals[2 * r], totals[2 * r + 1] = mp_sum(keeps[r]), mp_sum(aways[r])
        out_sums = mp_sum(out_kept), mp_sum(out_away)
        grads = stacked_sum(own, sib)
    else:
        both = chip_sum(own, sib)
        grads = plane_sum(both, BF16)
        out_pair = add_low(out_kept, swapped(after(out_away, totals), 1))
        out_total = add_low(out_pair, swapped(out_pair, 2))
        out_sums = out_total, swapped(out_total, 1)
    hidden = w_in.shape[1]
    grad_in, grad_back = grads[:, :hidden], grads[:, hidden:].T

    def column(j):
        return bundles[j // per], j % per * 3 * (full // groups)

    gres, gmix, g_gain2 = norm_bwd(meta, totals, resids, cotangent, vec)
    acc, own, sib = attn_bwd(
        meta, n_dp, 0, column(0)[1], gmix, heads[0], rest, column(0)[0], (attn_in, *atts)
    )
    if paired:
        both = chip_sum(own, sib)
        gmix = after(gmix, both, out_pair)
        piece = plane_sum(both, BF16).astype(BF16)
        pieces = [piece] + [
            lax.ppermute(piece, "mp", [(i, (i + d) % 4) for i in range(4)]) for d in range(1, 4)
        ]
    else:
        every = lax.all_gather(stacked_sum(own, sib).astype(BF16), "mp")
        pieces = [every[d] for d in range(groups)]
    grad_qkv, grad_out = assemble(meta, groups, paired, pieces)
    for j in range(1, groups - 1):
        (acc,) = attn_bwd(
            meta, n_dp, j, column(j)[1], gmix, heads[j], rest, column(j)[0], (acc,)
        )
    j = groups - 1
    if paired:
        gmix = after(gmix, piece, out_total, grads)
    grad_tokens, own, sib = attn_bwd(
        meta, n_dp, j, column(j)[1], gmix, heads[j], rest, column(j)[0],
        (acc, tokens, gres, vec, g_gain2, g_bback, g_bin),
    )
    small = plane_sum(chip_sum(own, sib), F32) if paired else stacked_sum(own, sib)
    output = finish(meta, resids, *out_sums, vec)
    return (
        output, grad_tokens, grad_qkv, grad_out, small[0], small[1], grad_in,
        small[3, : b_in.shape[0]], grad_back, small[2],
    )


def solution(mesh):
    in_specs = (
        P("dp", None),
        P("dp"),
        P("dp", None),
        P("dp", None),
        P("dp"),
        P("dp"),
        P("dp", "mp"),
        P(("mp", "dp")),
        P("mp", "dp"),
        P("dp"),
        P("dp", None),
    )
    out_specs = (
        P("dp", None),
        P("dp", None),
        P("dp", None),
        P("dp", None),
        P("dp"),
        P("dp"),
        P("dp", "mp"),
        P(("mp", "dp")),
        P("mp", "dp"),
        P("dp"),
    )
    body = functools.partial(per_device, mesh.shape["dp"], mesh.shape["mp"])
    return jax.shard_map(
        body, mesh=mesh, in_specs=in_specs, out_specs=out_specs, check_vma=False
    )
```

```python
import functools

import jax
import jax.numpy as jnp
from jax import lax
from jax.experimental import pallas as pl
from jax.experimental.pallas import tpu as pltpu
from jax.sharding import PartitionSpec as P

HD = 64
PAIR = 2 * HD
CHUNK = 256
EPS = 1e-05
PAIRED = 8
F32 = jnp.float32
BF16 = jnp.bfloat16
VMEM_LIMIT = 16 * 1024 * 1024
GELU_A = 0.7978845608028654
GELU_B = 0.044715


def cost(gflop, mbytes):
    return pl.CostEstimate(
        flops=int(gflop * 1e9), bytes_accessed=int(mbytes * 1e6), transcendentals=0
    )


ANY = pl.BlockSpec(memory_space=pl.ANY)
SMEM = pl.BlockSpec(memory_space=pltpu.SMEM)
VMEM = pl.BlockSpec(memory_space=pltpu.VMEM)


def nn(left, right):
    return jnp.dot(left, right, preferred_element_type=F32)


def nt(left, right):
    return lax.dot_general(left, right, (((1,), (1,)), ((), ())), preferred_element_type=F32)


def tn(left, right):
    return lax.dot_general(left, right, (((0,), (0,)), ((), ())), preferred_element_type=F32)


def normalize(values):
    centre = jnp.mean(values, -1, keepdims=True)
    centred = values - centre
    spread = jnp.mean(centred * centred, -1, keepdims=True)
    factor = lax.rsqrt(spread + EPS)
    return centred * factor, factor


def norm_back(grad, normed, factor):
    return factor * (
        grad
        - jnp.mean(grad, -1, keepdims=True)
        - normed * jnp.mean(grad * normed, -1, keepdims=True)
    )


def owner_of(base, k):
    near = 2 + 2 * (base & 1)
    chip = (0, near, 6 - near, 6)[k >> 1]
    return base ^ (chip if k & 1 == 0 else ((0, 6 - near, near, 6)[k >> 1] ^ 1))


def piece_copies(base, pieces, dst, sems, place=None, cols=None):
    copies = []
    size = dst.shape[0] // len(pieces)
    for k, piece in enumerate(pieces):
        if len(pieces) == 1:
            at = 0
        else:
            owner = owner_of(base, k)
            at = pl.multiple_of((owner if place is None else place(owner)) * size, size)
        start, width = (0, piece.shape[1]) if cols is None else cols
        copies.append(
            pltpu.make_async_copy(
                piece.at[pl.ds(0, size), pl.ds(start, width)], dst.at[pl.ds(at, size)], sems.at[k]
            )
        )
    return copies


def start_all(copies):
    for copy in copies:
        copy.start()


def wait_all(copies):
    for copy in copies:
        copy.wait()


def keep_of(length, start, rows):
    position = lax.broadcasted_iota(jnp.int32, (rows, 1), 0) + start
    return (position < length).astype(F32)


def lane_masks():
    lane = lax.broadcasted_iota(jnp.int32, (CHUNK, PAIR), 1)
    first = (lane < HD).astype(F32)
    return first.astype(BF16), (1.0 - first).astype(BF16)


def block_mask():
    row = lax.broadcasted_iota(jnp.int32, (PAIR, 2 * PAIR), 0)
    col = lax.broadcasted_iota(jnp.int32, (PAIR, 2 * PAIR), 1)
    return ((row < HD) == (col < PAIR)).astype(F32)


def split(state):
    high = state.astype(BF16)
    return high, (state - high.astype(F32)).astype(BF16)


def pair_of(arr, p):
    return arr[:, p * PAIR : (p + 1) * PAIR]


def prep_first_kernel(groups, per, vec_rows, meta, w_qkv, *refs):
    vectors, out = refs[:-1], refs[-1]
    rows, full = w_qkv.shape[0], w_qkv.shape[1] // 3
    width = full // groups
    for j in range(per):
        group = lax.rem(meta[1] + j, groups)
        for t in range(3):
            cols = pl.ds(pl.multiple_of(t * full + group * width, width), width)
            out[pl.ds(0, rows), pl.ds((3 * j + t) * width, width)] = w_qkv[:, cols].astype(BF16)
    if vec_rows:
        highs, mids, lows = [], [], []
        for vector in vectors:
            value = vector[...]
            high = value.astype(BF16).astype(F32)
            middle = (value - high).astype(BF16).astype(F32)
            highs.append(high)
            mids.append(middle)
            lows.append(value - high - middle)
        row = jnp.concatenate(highs + mids + lows, 1)
        out[pl.ds(rows, vec_rows), :] = jnp.broadcast_to(row, (vec_rows, row.shape[1])).astype(
            BF16
        )


def prep_first(meta, groups, per, vec_rows, w_qkv, vectors):
    rows, full = w_qkv.shape
    return pl.pallas_call(
        functools.partial(prep_first_kernel, groups, per, vec_rows),
        out_shape=jax.ShapeDtypeStruct((rows + vec_rows, per * full // groups), BF16),
        in_specs=[SMEM] + [VMEM] * (1 + len(vectors)),
        out_specs=VMEM,
        compiler_params=pltpu.CompilerParams(vmem_limit_bytes=VMEM_LIMIT),
        cost_estimate=cost(0.001, 3),
        name="prep_first",
    )(meta, w_qkv, *vectors)


def prep_rest_kernel(groups, per, bundles, meta, w_qkv, w_out, w_in, w_back, *outs):
    full = w_qkv.shape[1] // 3
    width = full // groups
    for b in range(bundles):
        for j in range(per):
            group = lax.rem(meta[1] + (b + 1) * per + j, groups)
            for t in range(3):
                cols = pl.ds(pl.multiple_of(t * full + group * width, width), width)
                outs[b][:, pl.ds((3 * j + t) * width, width)] = w_qkv[:, cols].astype(BF16)
    out = outs[bundles]
    hidden = w_in.shape[1]
    out[:, pl.ds(0, full)] = w_out[...].astype(BF16)
    out[:, pl.ds(full, hidden)] = w_in[...].astype(BF16)
    step = min(hidden, 256)
    for s in range(hidden // step):
        out[:, pl.ds(full + hidden + s * step, step)] = jnp.transpose(
            w_back[pl.ds(s * step, step), :]
        ).astype(BF16)


def prep_rest(meta, groups, per, w_qkv, w_out, w_in, w_back):
    rows, full = w_qkv.shape
    bundles = groups // per - 1
    shapes = [jax.ShapeDtypeStruct((rows, per * full // groups), BF16)] * bundles
    shapes.append(jax.ShapeDtypeStruct((rows, full // 3 + 2 * w_in.shape[1]), BF16))
    return pl.pallas_call(
        functools.partial(prep_rest_kernel, groups, per, bundles),
        out_shape=tuple(shapes),
        in_specs=[SMEM] + [VMEM] * 4,
        out_specs=(VMEM,) * len(shapes),
        compiler_params=pltpu.CompilerParams(vmem_limit_bytes=VMEM_LIMIT),
        cost_estimate=cost(0.001, 5),
        name="prep_rest",
    )(meta, w_qkv, w_out, w_in, w_back)


def attn_fwd_kernel(n_pieces, count_vec, start, meta, source, *refs):
    pieces = refs[:n_pieces]
    fq_out, fk_out, val_out, att_out, rden_out = refs[n_pieces : n_pieces + 5]
    rest = refs[n_pieces + 5 :]
    if count_vec:
        attn_in, vec_out, weight, sems, vec_scr, vec_sems = rest
    else:
        weight, sems = rest
        attn_in = source
    width = fq_out.shape[1]
    pairs = width // PAIR
    copies = piece_copies(meta[0], pieces, weight, sems, None, (start, 3 * width))
    count = source.shape[0] // CHUNK
    if count_vec:
        size = vec_out.shape[1] // n_pieces
        moves = [
            pltpu.make_async_copy(
                piece.at[pl.ds(size, vec_scr.shape[1])], vec_scr.at[k], vec_sems.at[k]
            )
            for k, piece in enumerate(pieces)
        ]
        start_all(moves)
        start_all(copies)
        for k, move in enumerate(moves):
            move.wait()
            value = vec_scr[k].astype(F32)[0:1]
            at = pl.ds(pl.multiple_of(owner_of(meta[0], k) * size, size), size)
            for a in range(count_vec):
                parts = [
                    value[:, (t * count_vec + a) * size : (t * count_vec + a + 1) * size]
                    for t in range(3)
                ]
                vec_out[a : a + 1, at] = parts[0] + parts[1] + parts[2]
        gain = vec_out[0:1, :]
        for c in range(count):
            rows = pl.ds(c * CHUNK, CHUNK)
            attn_in[rows, :] = (source[rows, :] * gain).astype(BF16)
    else:
        start_all(copies)
    wait_all(copies)
    mask_a, mask_b = lane_masks()
    blocks = block_mask()
    first = lax.broadcasted_iota(jnp.int32, (CHUNK, PAIR), 1) < HD
    causal = lax.broadcasted_iota(jnp.int32, (CHUNK, CHUNK), 0) >= lax.broadcasted_iota(
        jnp.int32, (CHUNK, CHUNK), 1
    )
    states = [None] * pairs
    for c in range(count):
        rows = pl.ds(c * CHUNK, CHUNK)
        proj = nn(attn_in[rows, :], weight[...])
        query, keys = proj[:, :width], proj[:, width : 2 * width]
        fq = jnp.where(query > 0, query + 1.0, jnp.exp(jnp.minimum(query, 0.0))).astype(BF16)
        fk = jnp.where(keys > 0, keys + 1.0, jnp.exp(jnp.minimum(keys, 0.0))).astype(BF16)
        val = proj[:, 2 * width :].astype(BF16)
        fq_out[rows, :] = fq
        fk_out[rows, :] = fk
        val_out[rows, :] = val
        for p in range(pairs):
            q, k, v = pair_of(fq, p), pair_of(fk, p), pair_of(val, p)
            v_a = v * mask_a + mask_b
            v_b = v * mask_b + mask_a
            s_a = jnp.where(causal, nt(q * mask_a, k), 0.0).astype(BF16)
            s_b = jnp.where(causal, nt(q * mask_b, k), 0.0).astype(BF16)
            r_a, r_b = nn(s_a, v_a), nn(s_b, v_b)
            if c > 0:
                high, low = split(states[p])
                past = nn(q, high) + nn(q, low)
                r_a = r_a + past[:, :PAIR]
                r_b = r_b + past[:, PAIR:]
            numer = jnp.where(first, r_a, r_b)
            denom = pltpu.roll(jnp.where(first, r_b, r_a), HD, axis=1)
            inverse = 1.0 / denom
            cols = pl.ds(p * PAIR, PAIR)
            att_out[rows, cols] = (numer * inverse).astype(BF16)
            rden_out[rows, cols] = inverse.astype(BF16)
            if c + 1 < count:
                new = tn(k, jnp.concatenate([v_a, v_b], 1)) * blocks
                states[p] = new if c == 0 else states[p] + new


def attn_fwd(meta, source, pieces, groups, position, count_vec):
    rows, full = source.shape
    width = full // groups
    n = len(pieces)
    shapes = [jax.ShapeDtypeStruct((rows, width), BF16)] * 5
    scratch = [pltpu.VMEM((full, 3 * width), BF16), pltpu.SemaphoreType.DMA((n,))]
    if count_vec:
        shapes += [
            jax.ShapeDtypeStruct((rows, full), BF16),
            jax.ShapeDtypeStruct((count_vec, full), F32),
        ]
        vec_rows = pieces[0].shape[0] - full // n
        scratch += [
            pltpu.VMEM((n, vec_rows, pieces[0].shape[1]), BF16),
            pltpu.SemaphoreType.DMA((n,)),
        ]
    return pl.pallas_call(
        functools.partial(attn_fwd_kernel, n, count_vec, position * 3 * width),
        out_shape=tuple(shapes),
        in_specs=[SMEM, VMEM] + [ANY] * n,
        out_specs=(VMEM,) * len(shapes),
        scratch_shapes=scratch,
        compiler_params=pltpu.CompilerParams(vmem_limit_bytes=VMEM_LIMIT),
        cost_estimate=cost(8, 6),
        name="attn_fwd",
    )(meta, source, *pieces)


def rest_copies(meta, which, pieces, dst, sems, groups):
    n = len(pieces)
    full = dst.shape[0]
    if which:
        hidden = dst.shape[1]
        cols = (full + (which - 1) * hidden, hidden)
        return piece_copies(meta[0], pieces, dst, sems.at[which], None, cols)
    width = full // groups
    if n == 1:
        found = []
        for j in range(groups):
            at = pl.multiple_of(lax.rem(meta[1] + j, groups) * width, width)
            found.append(
                pltpu.make_async_copy(
                    pieces[0].at[pl.ds(at, width), pl.ds(0, full)],
                    dst.at[pl.ds(j * width, width)],
                    sems.at[0, j],
                )
            )
        return found
    span = n // groups

    def turned(owner):
        group = lax.rem(owner // span - meta[1] + groups, groups)
        return group * span + lax.rem(owner, span)

    return piece_copies(meta[0], pieces, dst, sems.at[0], turned, (0, full))


def mlp_kernel(n_pieces, n_atts, groups, part, meta, *refs):
    atts = refs[:n_atts]
    tok, cot, vec, bias = refs[n_atts : n_atts + 4]
    pieces = refs[n_atts + 4 : n_atts + 4 + n_pieces]
    refs = refs[n_atts + 4 + n_pieces :]
    send_out, keep_out, hidden_out, gpre_out, min_out, resid_out = refs[:6]
    w_o, w_i, w_b, sems = refs[6:]
    i = pl.program_id(0)

    def loads(which):
        return rest_copies(meta, which, pieces, (w_o, w_i, w_b)[which], sems, groups)

    @pl.when(i == 0)
    def _():
        for which in range(3):
            start_all(loads(which))
        wait_all(loads(0))

    gain = vec[1:2, :]
    start = (2 * part + (i ^ (1 - meta[3]))) * CHUNK
    keep = keep_of(meta[2], start, CHUNK)
    g_low = (cot[...].astype(F32) * keep).astype(BF16)
    mixed = nn(jnp.concatenate([att[...] for att in atts], 1), w_o[...])
    resid = tok[...].astype(F32) + mixed
    resid_out[...] = resid
    normed, _ = normalize(resid)
    mlp_in = (normed * gain).astype(BF16)
    min_out[...] = mlp_in

    @pl.when(i == 0)
    def _():
        wait_all(loads(1))
        wait_all(loads(2))

    pre = nn(mlp_in, w_i[...]) + bias[...]
    square = pre * pre
    t = jnp.tanh(GELU_A * pre * (1.0 + GELU_B * square))
    half = 0.5 * (1.0 + t)
    hidden_out[...] = (pre * half).astype(BF16)
    slope = half + (0.5 * GELU_A) * pre * (1.0 - t * t) * (1.0 + (3.0 * GELU_B) * square)
    gpre = (nn(g_low, w_b[...]) * slope).astype(BF16)
    gpre_out[...] = gpre
    grad = nt(gpre, w_i[...]).astype(BF16)

    @pl.when(i == 0)
    def _():
        send_out[...] = grad

    @pl.when(i == 1)
    def _():
        keep_out[...] = grad


def mlp(meta, part, atts, groups, tokens, cotangent, vec, bias, pieces):
    n, n_atts = len(pieces), len(atts)
    rows = 2 * CHUNK
    width, hidden = tokens.shape[1], bias.shape[1]

    def rowed(cols, base):
        return pl.BlockSpec((CHUNK, cols), lambda i, m: (base + (i ^ (1 - m[3])), 0))

    def whole(shape):
        return pl.BlockSpec(shape, lambda i, m: (0, 0))

    shapes = [(CHUNK, width), (CHUNK, width), (rows, hidden), (rows, hidden), (rows, width)]
    return pl.pallas_call(
        functools.partial(mlp_kernel, n, n_atts, groups, part),
        out_shape=tuple(jax.ShapeDtypeStruct(shape, BF16) for shape in shapes)
        + (jax.ShapeDtypeStruct((rows, width), F32),),
        grid_spec=pltpu.PrefetchScalarGridSpec(
            num_scalar_prefetch=1,
            grid=(2,),
            in_specs=[rowed(a.shape[1], 2 * part) for a in atts]
            + [rowed(width, 2 * part)] * 2
            + [whole(vec.shape), whole(bias.shape)]
            + [ANY] * n,
            out_specs=(
                whole((CHUNK, width)),
                whole((CHUNK, width)),
                rowed(hidden, 0),
                rowed(hidden, 0),
                rowed(width, 0),
                rowed(width, 0),
            ),
            scratch_shapes=[
                pltpu.VMEM((width, width), BF16),
                pltpu.VMEM((width, hidden), BF16),
                pltpu.VMEM((width, hidden), BF16),
                pltpu.SemaphoreType.DMA((3, max(n, groups))),
            ],
        ),
        compiler_params=pltpu.CompilerParams(vmem_limit_bytes=VMEM_LIMIT),
        cost_estimate=cost(8, 16),
        name="mlp_fwd_bwd",
    )(meta, *atts, tokens, cotangent, vec, bias, *pieces)


def mlp_out_kernel(n_pieces, parts, meta, *refs):
    hiddens = refs[:parts]
    pieces = refs[parts : parts + n_pieces]
    send, keep, w_b, sems = refs[parts + n_pieces :]
    copies = rest_copies(meta, 2, pieces, w_b, sems, 1)
    start_all(copies)
    wait_all(copies)
    for c, out in enumerate((send, keep)):
        at = pl.multiple_of((c ^ (1 - meta[3])) * CHUNK, CHUNK)
        for r in range(parts):
            out[pl.ds(r * CHUNK, CHUNK), :] = nt(hiddens[r][pl.ds(at, CHUNK), :], w_b[...]).astype(
                BF16
            )


def mlp_out(meta, hiddens, pieces, width):
    n, parts = len(pieces), len(hiddens)
    hidden = hiddens[0].shape[1]
    return pl.pallas_call(
        functools.partial(mlp_out_kernel, n, parts),
        out_shape=(jax.ShapeDtypeStruct((parts * CHUNK, width), BF16),) * 2,
        in_specs=[SMEM] + [VMEM] * parts + [ANY] * n,
        out_specs=(VMEM,) * 2,
        scratch_shapes=[
            pltpu.VMEM((width, hidden), BF16),
            pltpu.SemaphoreType.DMA((3, n)),
        ],
        compiler_params=pltpu.CompilerParams(vmem_limit_bytes=VMEM_LIMIT),
        cost_estimate=cost(4, 8),
        name="mlp_out",
    )(meta, *hiddens, *pieces)


def offset_of(n_blocks, base, k, size):
    return pl.multiple_of((base ^ k) * size, size) if n_blocks == PAIRED else k * size


def spread(n_blocks, base, scratch, own, sib, start):
    size = own.shape[1]
    cols = pl.ds(start, scratch.shape[1])
    for k in range(n_blocks):
        at = offset_of(n_blocks, base, k, size)
        (own, sib)[k & 1][k >> 1, :, cols] = scratch[pl.ds(at, size), :]


def mlp_grads_kernel(n_blocks, parts, meta, *refs):
    hiddens, gpres, mins = (refs[a * parts : (a + 1) * parts] for a in range(3))
    cot = refs[3 * parts]
    own, sib, bin_out, bback_out, scratch, g_low = refs[3 * parts + 1 :]
    rows = hiddens[0].shape[0]
    total_in = total_back = None
    for r in range(parts):
        keep = keep_of(meta[2], r * rows, rows)
        g = cot[pl.ds(r * rows, rows), :].astype(F32) * keep
        g_low[pl.ds(r * rows, rows), :] = g.astype(BF16)
        back = jnp.sum(g, 0, keepdims=True)
        inner = jnp.sum(gpres[r][...].astype(F32), 0, keepdims=True)
        total_in = inner if total_in is None else total_in + inner
        total_back = back if total_back is None else total_back + back
    bin_out[...] = total_in
    bback_out[...] = total_back
    step = 256
    hidden = hiddens[0].shape[1]
    for s in range(scratch.shape[0] // step):
        cols = pl.ds(s * step, step)
        up = down = None
        for r in range(parts):
            part = tn(mins[r][:, cols], gpres[r][...])
            up = part if up is None else up + part
            part = tn(g_low[pl.ds(r * rows, rows), cols], hiddens[r][...])
            down = part if down is None else down + part
        scratch[cols, pl.ds(0, hidden)] = up.astype(BF16)
        scratch[cols, pl.ds(hidden, hidden)] = down.astype(BF16)
    spread(n_blocks, meta[0], scratch, own, sib, 0)


def mlp_grads(meta, n_blocks, hiddens, gpres, mins, cotangent):
    parts = len(hiddens)
    hidden, width = hiddens[0].shape[1], mins[0].shape[1]
    blocks = jax.ShapeDtypeStruct((n_blocks // 2, width // n_blocks, 2 * hidden), BF16)
    return pl.pallas_call(
        functools.partial(mlp_grads_kernel, n_blocks, parts),
        out_shape=(
            blocks,
            blocks,
            jax.ShapeDtypeStruct((1, hidden), F32),
            jax.ShapeDtypeStruct((1, width), F32),
        ),
        in_specs=[SMEM] + [VMEM] * (3 * parts + 1),
        out_specs=(VMEM,) * 4,
        scratch_shapes=[
            pltpu.VMEM((width, 2 * hidden), BF16),
            pltpu.VMEM(cotangent.shape, BF16),
        ],
        compiler_params=pltpu.CompilerParams(vmem_limit_bytes=VMEM_LIMIT),
        cost_estimate=cost(8, 16),
        name="mlp_grads",
    )(meta, *hiddens, *gpres, *mins, cotangent)


def norm_bwd_kernel(parts, meta, *refs):
    totals = refs[: 2 * parts]
    resids = refs[2 * parts : 3 * parts]
    cot, vec, gres_out, gmix_out, gain_out = refs[3 * parts :]
    i = pl.program_id(0)
    chunk = 2 * (i // 2) + (lax.rem(i, 2) ^ meta[3])
    keep = keep_of(meta[2], chunk * CHUNK, CHUNK)

    @pl.when(i == 0)
    def _():
        gain_out[...] = jnp.zeros_like(gain_out)

    for r in range(parts):
        for h in range(2):

            @pl.when(i == 2 * r + h)
            def _():
                grad = totals[2 * r + h][...].astype(F32)
                normed, factor = normalize(resids[r][...])
                gain_out[...] += jnp.sum(grad * normed, 0, keepdims=True)
                gres = cot[...].astype(F32) * keep + norm_back(
                    grad * vec[1:2, :], normed, factor
                )
                gres_out[...] = gres
                gmix_out[...] = gres.astype(BF16)


def norm_bwd(meta, totals, resids, cotangent, vec):
    parts = len(resids)
    rows, full = cotangent.shape

    def whole(shape):
        return pl.BlockSpec(shape, lambda i, m: (0, 0))

    def inner(r):
        def index(i, m):
            bit = lax.rem(jnp.clip(i - 2 * r, 0, 1), 2)
            return (bit ^ m[3], 0)

        return pl.BlockSpec((CHUNK, full), index)

    rowed = pl.BlockSpec((CHUNK, full), lambda i, m: (2 * (i // 2) + (lax.rem(i, 2) ^ m[3]), 0))
    return pl.pallas_call(
        functools.partial(norm_bwd_kernel, parts),
        out_shape=(
            jax.ShapeDtypeStruct((rows, full), F32),
            jax.ShapeDtypeStruct((rows, full), BF16),
            jax.ShapeDtypeStruct((1, full), F32),
        ),
        grid_spec=pltpu.PrefetchScalarGridSpec(
            num_scalar_prefetch=1,
            grid=(2 * parts,),
            in_specs=[whole(t.shape) for t in totals]
            + [inner(r) for r in range(parts)]
            + [rowed, whole(vec.shape)],
            out_specs=(rowed, rowed, whole((1, full))),
        ),
        compiler_params=pltpu.CompilerParams(vmem_limit_bytes=VMEM_LIMIT),
        cost_estimate=cost(1, 16),
        name="norm_bwd",
    )(meta, *totals, *resids, cotangent, vec)


def group_rows(meta, group, width, pieces, dst, sems, start):
    full = dst.shape[1]
    if len(pieces) == 1:
        at = pl.multiple_of(group * width, width)
        copy = pltpu.make_async_copy(
            pieces[0].at[pl.ds(at, width), pl.ds(0, full)], dst, sems.at[0]
        )
        return copy.start() if start else copy.wait()
    size = pieces[0].shape[0]
    for part in range(width // size):
        wanted = group * (width // size) + part
        target = dst.at[pl.ds(part * size, size)]
        if not start:
            pltpu.make_async_copy(
                pieces[0].at[:, pl.ds(0, full)], target, sems.at[part]
            ).wait()
            continue
        for k, piece in enumerate(pieces):

            @pl.when(wanted == owner_of(meta[0], k))
            def _():
                pltpu.make_async_copy(
                    piece.at[:, pl.ds(0, full)], target, sems.at[part]
                ).start()


def attn_bwd_kernel(shape, meta, *refs):
    n, groups, position, start, n_atts, n_vectors, n_blocks = shape
    is_first, is_last = position == 0, position == groups - 1
    refs = list(refs)

    def take(count):
        found = refs[:count]
        del refs[:count]
        return found

    gmix, fq, fk, val, att, rden = take(6)
    (acc_in,) = take(1) if not is_first else (None,)
    attn_in, *atts = take(1 + n_atts) if is_first else (None,)
    tok, gres, vec, *vectors = take(3 + n_vectors) if is_last else (None, None, None)
    pieces_o, pieces_w = take(n), take(n)
    (acc_out,) = take(1)
    own, sib = take(2) if is_first or is_last else (None, None)
    w_o, w_q, state_scr, later, sems_o, sems_w = take(6)
    width = fq.shape[1]
    pairs = width // PAIR
    full = gmix.shape[1]
    i = pl.program_id(0)
    count = fk.shape[0] // CHUNK
    c = count - 1 - i
    place = meta[1]
    group = lax.rem(place + position, groups)
    mask_a, mask_b = lane_masks()
    blocks = block_mask()

    def weight_copies():
        return piece_copies(meta[0], pieces_w, w_q, sems_w, None, (start, 3 * width))

    def side_copies():
        found = [pltpu.make_async_copy(attn_in, ain_scr, side_sems.at[0])]
        for a in range(n_atts):
            found.append(
                pltpu.make_async_copy(
                    atts[a], att_scr.at[:, pl.ds(a * width, width)], side_sems.at[a + 1]
                )
            )
        return found

    if is_first:
        gproj_scr, gcol_scr, ain_scr, att_scr, product, side_sems = take(6)
    if is_last:
        (gain_scr,) = take(1)

    @pl.when(i == 0)
    def _():
        group_rows(meta, group, width, pieces_o, w_o, sems_o, True)
        start_all(weight_copies())
        if is_first:
            start_all(side_copies())
        if is_last:
            gain_scr[...] = jnp.zeros_like(gain_scr)
        later[...] = jnp.zeros_like(later)
        for p in range(pairs):
            state = jnp.zeros((PAIR, 2 * PAIR), F32)
            for s in range(count):
                high, low = split(state)
                state_scr[s, p, 0] = high
                state_scr[s, p, 1] = low
                if s + 1 < count:
                    rows, cols = pl.ds(s * CHUNK, CHUNK), pl.ds(p * PAIR, PAIR)
                    v = val[rows, cols]
                    aug = jnp.concatenate([v * mask_a + mask_b, v * mask_b + mask_a], 1)
                    state = state + tn(fk[rows, cols], aug) * blocks
        group_rows(meta, group, width, pieces_o, w_o, sems_o, False)
        wait_all(weight_copies())

    first = lax.broadcasted_iota(jnp.int32, (CHUNK, PAIR), 1) < HD
    row = lax.broadcasted_iota(jnp.int32, (CHUNK, CHUNK), 0)
    col = lax.broadcasted_iota(jnp.int32, (CHUNK, CHUNK), 1)
    causal, causal_t = row >= col, row <= col
    head_row = lax.broadcasted_iota(jnp.int32, (width, width), 0) // HD
    head_col = lax.broadcasted_iota(jnp.int32, (width, width), 1) // HD
    head_sum = (head_row == head_col).astype(F32).astype(BF16)
    rows = pl.ds(pl.multiple_of(c * CHUNK, CHUNK), CHUNK)
    grad_att = nt(gmix[...], w_o[...])
    inverse = rden[...].astype(F32)
    gnum = (grad_att * inverse).astype(BF16)
    dots = nn((grad_att * att[...].astype(F32)).astype(BF16), head_sum)
    gden = (-dots * inverse).astype(BF16).astype(F32)
    found_q, found_k, found_v = [], [], []
    for p in range(pairs):
        cols = pl.ds(p * PAIR, PAIR)
        q, k, v = fq[:, cols], fk[rows, cols], val[rows, cols]
        num = pair_of(gnum, p)
        den = (pltpu.roll(pair_of(gden, p), HD, axis=1) * (1.0 / HD)).astype(BF16)
        n_a, n_b = num * mask_a + den * mask_b, num * mask_b + den * mask_a
        q_a, q_b = q * mask_a, q * mask_b
        v_a, v_b = v * mask_a + mask_b, v * mask_b + mask_a
        n_cat = jnp.concatenate([n_a, n_b], 1)
        v_cat = jnp.concatenate([v_a, v_b], 1)
        st_a = jnp.where(causal_t, nt(k, q_a), 0.0).astype(BF16)
        st_b = jnp.where(causal_t, nt(k, q_b), 0.0).astype(BF16)
        gs_a = jnp.where(causal, nt(n_a, v_a), 0.0).astype(BF16)
        gs_b = jnp.where(causal, nt(n_b, v_b), 0.0).astype(BF16)
        gt_a = jnp.where(causal_t, nt(v_a, n_a), 0.0).astype(BF16)
        gt_b = jnp.where(causal_t, nt(v_b, n_b), 0.0).astype(BF16)
        high, low = split(later[p])
        past = nn(k, high) + nn(k, low)
        gq = nn(gs_a, k * mask_a) + nn(gs_b, k * mask_b)
        gq = gq + nt(n_cat, state_scr[c, p, 0]) + nt(n_cat, state_scr[c, p, 1])
        gk = nn(gt_a, q_a) + nn(gt_b, q_b) + nt(v_cat, high) + nt(v_cat, low)
        gv = nn(st_a, num * mask_a) + nn(st_b, num * mask_b)
        gv = gv + jnp.where(first, past[:, :PAIR], past[:, PAIR:])
        later[p] = later[p] + tn(q, n_cat) * blocks
        found_q.append((gq * jnp.minimum(q.astype(F32), 1.0)).astype(BF16))
        found_k.append((gk * jnp.minimum(k.astype(F32), 1.0)).astype(BF16))
        found_v.append(gv.astype(BF16))
    gproj = jnp.concatenate(found_q + found_k + found_v, 1)
    grad = nt(gproj, w_q[...])
    if not is_first:
        grad = grad + acc_in[...]
    if not is_last:
        acc_out[...] = grad
    else:
        normed, factor = normalize(tok[...].astype(F32))
        gain_scr[...] += jnp.sum(grad * normed, 0, keepdims=True)
        acc_out[...] = gres[...] + norm_back(grad * vec[0:1, :], normed, factor)

        @pl.when(i == count - 1)
        def _():
            for a, source in enumerate([gain_scr] + vectors):
                size = source.shape[1] // n_blocks
                for k in range(n_blocks):
                    at = offset_of(n_blocks, meta[0], k, size)
                    (own, sib)[k & 1][k >> 1, a : a + 1, pl.ds(0, size)] = source[
                        :, pl.ds(at, size)
                    ]

    if is_first:
        gproj_scr[rows, :] = gproj
        gcol_scr[rows, :] = gmix[:, pl.ds(pl.multiple_of(place * width, width), width)]

        @pl.when(i == count - 1)
        def _():
            wait_all(side_copies())
            for s in range(full // 256):
                piece = pl.ds(s * 256, 256)
                product[piece, pl.ds(0, 3 * width)] = tn(
                    ain_scr[:, s * 256 : (s + 1) * 256], gproj_scr[...]
                ).astype(BF16)
            for j in range(groups):
                at = pl.multiple_of(lax.rem(place + j, groups) * width, width)
                product[pl.ds(at, width), pl.ds(3 * width, width)] = tn(
                    att_scr[:, j * width : (j + 1) * width], gcol_scr[...]
                ).astype(BF16)
            spread(n_blocks, meta[0], product, own, sib, 0)


def attn_bwd(meta, n_blocks, position, start, gmix, heads, pieces_o, pieces_w, extra):
    n = len(pieces_o)
    rows, full = gmix.shape
    width = heads[0].shape[1]
    groups = full // width
    count = rows // CHUNK
    is_first, is_last = position == 0, position == groups - 1

    def rowed(cols):
        return pl.BlockSpec((CHUNK, cols), lambda i: (count - 1 - i, 0))

    def whole(shape):
        return pl.BlockSpec(shape, lambda i: (0,) * len(shape))

    specs = [rowed(full), rowed(width), whole((rows, width)), whole((rows, width))]
    specs += [rowed(width), rowed(width)]
    n_atts = n_vectors = 0
    if is_first:
        n_atts = len(extra) - 1
        specs += [ANY] * len(extra)
    else:
        specs += [rowed(full)]
    if is_last:
        n_vectors = len(extra) - 4
        specs += [rowed(full), rowed(full)] + [whole(v.shape) for v in extra[3:]]
    shapes, outs = [jax.ShapeDtypeStruct((rows, full), F32)], [rowed(full)]
    scratch = [
        pltpu.VMEM((width, full), BF16),
        pltpu.VMEM((full, 3 * width), BF16),
        pltpu.VMEM((count, width // PAIR, 2, PAIR, 2 * PAIR), BF16),
        pltpu.VMEM((width // PAIR, PAIR, 2 * PAIR), F32),
        pltpu.SemaphoreType.DMA((max(1, width * n // full),)),
        pltpu.SemaphoreType.DMA((n,)),
    ]
    if is_first:
        blocks = (n_blocks // 2, full // n_blocks, 4 * width)
        shapes += [jax.ShapeDtypeStruct(blocks, BF16)] * 2
        outs += [whole(blocks)] * 2
        scratch += [
            pltpu.VMEM((rows, 3 * width), BF16),
            pltpu.VMEM((rows, width), BF16),
            pltpu.VMEM((rows, full), BF16),
            pltpu.VMEM((rows, full), BF16),
            pltpu.VMEM((full, 4 * width), BF16),
            pltpu.SemaphoreType.DMA((n_atts + 1,)),
        ]
    if is_last:
        small = (n_blocks // 2, 4, full // n_blocks)
        shapes += [jax.ShapeDtypeStruct(small, F32)] * 2
        outs += [whole(small)] * 2
        scratch += [pltpu.VMEM((1, full), F32)]
    shape = (n, groups, position, start, n_atts, n_vectors, n_blocks)
    return pl.pallas_call(
        functools.partial(attn_bwd_kernel, shape),
        grid=(count,),
        out_shape=tuple(shapes),
        in_specs=[SMEM] + specs + [ANY] * (2 * n),
        out_specs=tuple(outs),
        scratch_shapes=scratch,
        compiler_params=pltpu.CompilerParams(vmem_limit_bytes=VMEM_LIMIT),
        cost_estimate=cost(10, 7),
        name="attn_bwd",
    )(meta, gmix, *heads, *extra, *pieces_o, *pieces_w)


def finish_kernel(parts, meta, *refs):
    resids = refs[:parts]
    kept, other, vec, out = refs[parts:]
    bias = vec[3:4, :]
    for r in range(parts):
        for source, h in ((kept, 0), (other, 1)):
            inner = pl.multiple_of((h ^ meta[3]) * CHUNK, CHUNK)
            at = pl.multiple_of(r * 2 * CHUNK + inner, CHUNK)
            summed = source[pl.ds(r * CHUNK, CHUNK), :].astype(F32)
            total = resids[r][pl.ds(inner, CHUNK), :] + (summed + bias)
            keep = keep_of(meta[2], at, CHUNK)
            out[pl.ds(at, CHUNK), :] = (total * keep).astype(BF16)


def finish(meta, resids, kept, other, vec):
    rows, width = 2 * CHUNK * len(resids), kept.shape[1]
    return pl.pallas_call(
        functools.partial(finish_kernel, len(resids)),
        out_shape=jax.ShapeDtypeStruct((rows, width), BF16),
        in_specs=[SMEM] + [VMEM] * (len(resids) + 3),
        out_specs=VMEM,
        compiler_params=pltpu.CompilerParams(vmem_limit_bytes=VMEM_LIMIT),
        cost_estimate=cost(0.01, 8),
        name="finish",
    )(meta, *resids, kept, other, vec)


def assemble_kernel(groups, turned, meta, *refs):
    pieces, (qkv, out) = refs[:-2], refs[-2:]
    width = out.shape[1] // groups
    for d, piece in enumerate(pieces):
        group = meta[1] ^ d if turned else d
        for t in range(4):
            value = piece[:, pl.ds(t * width, width)].astype(F32)
            start = t % 3 * groups * width + group * width
            at = pl.ds(pl.multiple_of(start, width), width)
            (out if t == 3 else qkv)[:, at] = value


def assemble(meta, groups, turned, pieces):
    rows, width = pieces[0].shape[0], pieces[0].shape[1] // 4
    return pl.pallas_call(
        functools.partial(assemble_kernel, groups, turned),
        out_shape=(
            jax.ShapeDtypeStruct((rows, 3 * groups * width), F32),
            jax.ShapeDtypeStruct((rows, groups * width), F32),
        ),
        in_specs=[SMEM] + [VMEM] * len(pieces),
        out_specs=(VMEM,) * 2,
        compiler_params=pltpu.CompilerParams(vmem_limit_bytes=VMEM_LIMIT),
        cost_estimate=cost(0.01, 3),
        name="assemble",
    )(meta, *pieces)


def send(arr, move):
    return lax.ppermute(arr, "dp", [(i, move(i)) for i in range(PAIRED)])


def near(i):
    return i ^ (4 if i & 1 else 2)


def far(i):
    return i ^ (2 if i & 1 else 4)


def across(i):
    return i ^ 1


def after(arrs, *deps):
    return lax.optimization_barrier((arrs, deps))[0]


def gather_pieces(arr):
    one, two = send(arr, near), send(arr, far)
    three = send(one, far)
    pieces = []
    for piece in (arr, one, two, three):
        pieces += [piece, send(piece, across)]
    return pieces


def chip_sum(own, sib):
    return own.astype(F32) + send(sib, across).astype(F32)


def plane_sum(both, kind):
    total = both[0]
    for k in range(1, PAIRED // 2):
        moved = send(both[k].astype(kind), lambda i, k=k: i ^ (2 * k))
        total = total + moved.astype(F32)
    return total


def swapped(arr, bits):
    return lax.ppermute(arr, "mp", [(i, i ^ bits) for i in range(4)])


def add_low(left, right):
    return (left.astype(F32) + right.astype(F32)).astype(BF16)


def per_device(
    n_dp, n_mp, tokens, lengths, w_qkv, w_out, ln1_gain, ln2_gain, w_in, b_in, w_back, b_back,
    cotangent,
):
    rows, full = tokens.shape
    groups = n_mp
    per = 2
    paired = n_dp == PAIRED and n_mp == 4
    index = lax.axis_index("dp").astype(jnp.int32)
    place = lax.axis_index("mp").astype(jnp.int32)
    zero = jnp.zeros_like(index)
    meta = jnp.stack(
        [index if paired else zero, place, lengths[0], (place & 1) if paired else zero]
    )
    vectors = [v[None] for v in (ln1_gain, ln2_gain, b_in, b_back)]

    def gather(arr, axis=0):
        return lax.all_gather(arr, "dp", axis=axis, tiled=True)

    first_sent = prep_first(
        meta, groups, per, 16 if paired else 0, w_qkv, vectors if paired else ()
    )
    normed_one, _ = normalize(tokens.astype(F32))
    parts = rows // (2 * CHUNK)
    found, totals = [None] * parts, [None] * (2 * parts)

    if not paired:
        sent = [first_sent] + list(prep_rest(meta, groups, per, w_qkv, w_out, w_in, w_back))
        gathered = [[gather(arr)] for arr in sent]
        bundles, rest = gathered[:-1], gathered[-1]
        gain_one, gain_two, bias, bias_back = (gather(v, 1) for v in vectors)
        attn_in = (normed_one * gain_one).astype(BF16)
        vec = jnp.concatenate([gain_one, gain_two, gain_two, bias_back], 0)
        heads = [
            attn_fwd(meta, attn_in, bundles[j // per], groups, j % per, 0) for j in range(groups)
        ]
    else:
        bundles = [gather_pieces(first_sent)]
        raw = after((w_qkv, w_out, w_in, w_back), bundles[0][1])
        second, third = prep_rest(meta, groups, per, *raw)
        bundles.append(gather_pieces(second))
        rest = gather_pieces(after(third, bundles[0][2]))
        heads = [attn_fwd(meta, after(normed_one, bundles[1][2]), bundles[0], groups, 0, 4)]
        attn_in, vec = heads[0][5:]
        bias = vec[2:3]
        heads.append(attn_fwd(meta, attn_in, bundles[0], groups, 1, 0))
        attn_in = after(attn_in, rest[2])
        heads.append(attn_fwd(meta, attn_in, bundles[1], groups, 0, 0))
        heads.append(attn_fwd(meta, attn_in, bundles[1], groups, 1, 0))
    heads = [h[:5] for h in heads]
    atts = [h[3] for h in heads]

    for r in reversed(range(parts)):
        found[r] = mlp(meta, r, atts, groups, tokens, cotangent, vec, bias, rest)
    aways, keeps, hiddens, gpres, mins, resids = (list(x) for x in zip(*found))
    if paired:
        pairs = [None] * parts
        for r in reversed(range(parts)):
            pairs[r] = add_low(keeps[r], swapped(aways[r], 1))
        for r in reversed(range(parts)):
            totals[2 * r] = add_low(pairs[r], swapped(pairs[r], 2))
            totals[2 * r + 1] = swapped(totals[2 * r], 1)
    wide_own, wide_sib, g_bin, g_bback = mlp_grads(meta, n_dp, hiddens, gpres, mins, cotangent)
    out_away, out_kept = mlp_out(meta, hiddens, rest, full)

    def stacked_sum(own, sib):
        both = jnp.stack([own, sib], 1).reshape((n_dp,) + own.shape[1:])
        return lax.psum_scatter(both.astype(F32), "dp", scatter_dimension=0)

    def mp_sum(arr):
        return lax.psum(arr.astype(F32), "mp").astype(BF16)

    if not paired:
        for r in range(parts):
            totals[2 * r], totals[2 * r + 1] = mp_sum(keeps[r]), mp_sum(aways[r])
        out_sums = mp_sum(out_kept), mp_sum(out_away)
        grads = stacked_sum(wide_own, wide_sib)
    else:
        out_pair = add_low(out_kept, swapped(after(out_away, pairs[0]), 1))
        totals = after(totals, out_pair)
        got = send(wide_sib, across)

    def column(j):
        return bundles[j // per], j % per * 3 * (full // groups)

    gres, gmix, g_gain2 = norm_bwd(meta, totals, resids, cotangent, vec)
    acc, own, sib = attn_bwd(
        meta, n_dp, 0, column(0)[1], gmix, heads[0], rest, column(0)[0], (attn_in, *atts)
    )
    if paired:
        out_total = add_low(out_pair, swapped(out_pair, 2))
        both = chip_sum(own, after(sib, out_total))
        gmix = after(gmix, both)
        piece = plane_sum(both, BF16).astype(BF16)
        out_sums = out_total, swapped(out_total, 1)
        second = swapped(piece, 2)
        pieces = [piece, swapped(piece, 1), second, swapped(second, 1)]
        away = after(add_low(wide_own[1::2], got[1::2]), piece)
        kept = wide_own[::2].astype(F32) + got[::2].astype(F32)
        kept = kept + send(away, lambda i: i ^ 2).astype(F32)
        low = after(kept[1].astype(BF16), second)
        grads = kept[0] + send(low, lambda i: i ^ 4).astype(F32)
    else:
        every = lax.all_gather(stacked_sum(own, sib).astype(BF16), "mp")
        pieces = [every[d] for d in range(groups)]
    grad_qkv, grad_out = assemble(meta, groups, paired, pieces)
    for j in range(1, groups - 1):
        if paired and j == groups - 2:
            gmix = after(gmix, piece, out_total)
        (acc,) = attn_bwd(
            meta, n_dp, j, column(j)[1], gmix, heads[j], rest, column(j)[0], (acc,)
        )
    j = groups - 1
    if paired:
        gmix = after(gmix, second)
    grad_tokens, own, sib = attn_bwd(
        meta, n_dp, j, column(j)[1], gmix, heads[j], rest, column(j)[0],
        (acc, tokens, gres, vec, g_gain2, g_bback, g_bin),
    )
    if paired:
        small = plane_sum(chip_sum(own, after(sib, out_sums, pieces)), F32)
    else:
        small = stacked_sum(own, sib)
    output = finish(meta, resids, *out_sums, after(vec, acc))
    hidden = w_in.shape[1]
    grad_in, grad_back = grads[:, :hidden], grads[:, hidden:].T
    return (
        output, grad_tokens, grad_qkv, grad_out, small[0], small[1], grad_in,
        small[3, : b_in.shape[0]], grad_back, small[2],
    )


def solution(mesh):
    in_specs = (
        P("dp", None),
        P("dp"),
        P("dp", None),
        P("dp", None),
        P("dp"),
        P("dp"),
        P("dp", "mp"),
        P(("mp", "dp")),
        P("mp", "dp"),
        P("dp"),
        P("dp", None),
    )
    out_specs = (
        P("dp", None),
        P("dp", None),
        P("dp", None),
        P("dp", None),
        P("dp"),
        P("dp"),
        P("dp", "mp"),
        P(("mp", "dp")),
        P("mp", "dp"),
        P("dp"),
    )
    body = functools.partial(per_device, mesh.shape["dp"], mesh.shape["mp"])
    return jax.shard_map(
        body, mesh=mesh, in_specs=in_specs, out_specs=out_specs, check_vma=False
    )
```

```python
import functools

import jax
import jax.numpy as jnp
from jax import lax
from jax.experimental import pallas as pl
from jax.experimental.pallas import tpu as pltpu
from jax.sharding import PartitionSpec as P

HD = 64
PAIR = 2 * HD
CHUNK = 256
EPS = 1e-05
PAIRED = 8
F32 = jnp.float32
BF16 = jnp.bfloat16
VMEM_LIMIT = 16 * 1024 * 1024
GELU_A = 0.7978845608028654
GELU_B = 0.044715


def cost(gflop, mbytes):
    return pl.CostEstimate(
        flops=int(gflop * 1e9), bytes_accessed=int(mbytes * 1e6), transcendentals=0
    )


ANY = pl.BlockSpec(memory_space=pl.ANY)
SMEM = pl.BlockSpec(memory_space=pltpu.SMEM)
VMEM = pl.BlockSpec(memory_space=pltpu.VMEM)


def nn(left, right):
    return jnp.dot(left, right, preferred_element_type=F32)


def nt(left, right):
    return lax.dot_general(left, right, (((1,), (1,)), ((), ())), preferred_element_type=F32)


def tn(left, right):
    return lax.dot_general(left, right, (((0,), (0,)), ((), ())), preferred_element_type=F32)


def normalize(values):
    centre = jnp.mean(values, -1, keepdims=True)
    centred = values - centre
    spread = jnp.mean(centred * centred, -1, keepdims=True)
    factor = lax.rsqrt(spread + EPS)
    return centred * factor, factor


def norm_back(grad, normed, factor):
    return factor * (
        grad
        - jnp.mean(grad, -1, keepdims=True)
        - normed * jnp.mean(grad * normed, -1, keepdims=True)
    )


def owner_of(base, k):
    near = 2 + 2 * (base & 1)
    chip = (0, near, 6 - near, 6)[k >> 1]
    return base ^ (chip if k & 1 == 0 else ((0, 6 - near, near, 6)[k >> 1] ^ 1))


def piece_copies(base, pieces, dst, sems, place=None, cols=None):
    copies = []
    size = dst.shape[0] // len(pieces)
    for k, piece in enumerate(pieces):
        if len(pieces) == 1:
            at = 0
        else:
            owner = owner_of(base, k)
            at = pl.multiple_of((owner if place is None else place(owner)) * size, size)
        start, width = (0, piece.shape[1]) if cols is None else cols
        copies.append(
            pltpu.make_async_copy(
                piece.at[pl.ds(0, size), pl.ds(start, width)], dst.at[pl.ds(at, size)], sems.at[k]
            )
        )
    return copies


def start_all(copies):
    for copy in copies:
        copy.start()


def wait_all(copies):
    for copy in copies:
        copy.wait()


def keep_of(length, start, rows):
    position = lax.broadcasted_iota(jnp.int32, (rows, 1), 0) + start
    return (position < length).astype(F32)


def lane_masks():
    lane = lax.broadcasted_iota(jnp.int32, (CHUNK, PAIR), 1)
    first = (lane < HD).astype(F32)
    return first.astype(BF16), (1.0 - first).astype(BF16)


def block_mask():
    row = lax.broadcasted_iota(jnp.int32, (PAIR, 2 * PAIR), 0)
    col = lax.broadcasted_iota(jnp.int32, (PAIR, 2 * PAIR), 1)
    return ((row < HD) == (col < PAIR)).astype(F32)


def split(state):
    high = state.astype(BF16)
    return high, (state - high.astype(F32)).astype(BF16)


def pair_of(arr, p):
    return arr[:, p * PAIR : (p + 1) * PAIR]


def prep_first_kernel(groups, per, vec_rows, meta, w_qkv, *refs):
    vectors, out = refs[:-1], refs[-1]
    rows, full = w_qkv.shape[0], w_qkv.shape[1] // 3
    width = full // groups
    for j in range(per):
        group = lax.rem(meta[1] + j, groups)
        for t in range(3):
            cols = pl.ds(pl.multiple_of(t * full + group * width, width), width)
            out[pl.ds(0, rows), pl.ds((3 * j + t) * width, width)] = w_qkv[:, cols].astype(BF16)
    if vec_rows:
        highs, mids, lows = [], [], []
        for vector in vectors:
            value = vector[...]
            high = value.astype(BF16).astype(F32)
            middle = (value - high).astype(BF16).astype(F32)
            highs.append(high)
            mids.append(middle)
            lows.append(value - high - middle)
        row = jnp.concatenate(highs + mids + lows, 1)
        out[pl.ds(rows, vec_rows), :] = jnp.broadcast_to(row, (vec_rows, row.shape[1])).astype(
            BF16
        )


def prep_first(meta, groups, per, vec_rows, w_qkv, vectors):
    rows, full = w_qkv.shape
    return pl.pallas_call(
        functools.partial(prep_first_kernel, groups, per, vec_rows),
        out_shape=jax.ShapeDtypeStruct((rows + vec_rows, per * full // groups), BF16),
        in_specs=[SMEM] + [VMEM] * (1 + len(vectors)),
        out_specs=VMEM,
        compiler_params=pltpu.CompilerParams(vmem_limit_bytes=VMEM_LIMIT),
        cost_estimate=cost(0.001, 3),
        name="prep_first",
    )(meta, w_qkv, *vectors)


def prep_rest_kernel(groups, per, bundles, meta, w_qkv, w_out, w_in, w_back, *outs):
    full = w_qkv.shape[1] // 3
    width = full // groups
    for b in range(bundles):
        for j in range(per):
            group = lax.rem(meta[1] + (b + 1) * per + j, groups)
            for t in range(3):
                cols = pl.ds(pl.multiple_of(t * full + group * width, width), width)
                outs[b][:, pl.ds((3 * j + t) * width, width)] = w_qkv[:, cols].astype(BF16)
    out = outs[bundles]
    hidden = w_in.shape[1]
    out[:, pl.ds(0, full)] = w_out[...].astype(BF16)
    out[:, pl.ds(full, hidden)] = w_in[...].astype(BF16)
    step = min(hidden, 256)
    for s in range(hidden // step):
        out[:, pl.ds(full + hidden + s * step, step)] = jnp.transpose(
            w_back[pl.ds(s * step, step), :]
        ).astype(BF16)


def prep_rest(meta, groups, per, w_qkv, w_out, w_in, w_back):
    rows, full = w_qkv.shape
    bundles = groups // per - 1
    shapes = [jax.ShapeDtypeStruct((rows, per * full // groups), BF16)] * bundles
    shapes.append(jax.ShapeDtypeStruct((rows, full // 3 + 2 * w_in.shape[1]), BF16))
    return pl.pallas_call(
        functools.partial(prep_rest_kernel, groups, per, bundles),
        out_shape=tuple(shapes),
        in_specs=[SMEM] + [VMEM] * 4,
        out_specs=(VMEM,) * len(shapes),
        compiler_params=pltpu.CompilerParams(vmem_limit_bytes=VMEM_LIMIT),
        cost_estimate=cost(0.001, 5),
        name="prep_rest",
    )(meta, w_qkv, w_out, w_in, w_back)


def attn_fwd_kernel(n_pieces, count_vec, start, meta, source, *refs):
    pieces = refs[:n_pieces]
    fq_out, fk_out, val_out, att_out, rden_out = refs[n_pieces : n_pieces + 5]
    rest = refs[n_pieces + 5 :]
    if count_vec:
        attn_in, vec_out, weight, sems, vec_scr, vec_sems = rest
    else:
        weight, sems = rest
        attn_in = source
    width = fq_out.shape[1]
    pairs = width // PAIR
    copies = piece_copies(meta[0], pieces, weight, sems, None, (start, 3 * width))
    count = source.shape[0] // CHUNK
    if count_vec:
        size = vec_out.shape[1] // n_pieces
        moves = [
            pltpu.make_async_copy(
                piece.at[pl.ds(size, vec_scr.shape[1])], vec_scr.at[k], vec_sems.at[k]
            )
            for k, piece in enumerate(pieces)
        ]
        start_all(moves)
        start_all(copies)
        for k, move in enumerate(moves):
            move.wait()
            value = vec_scr[k].astype(F32)[0:1]
            at = pl.ds(pl.multiple_of(owner_of(meta[0], k) * size, size), size)
            for a in range(count_vec):
                parts = [
                    value[:, (t * count_vec + a) * size : (t * count_vec + a + 1) * size]
                    for t in range(3)
                ]
                vec_out[a : a + 1, at] = parts[0] + parts[1] + parts[2]
        gain = vec_out[0:1, :]
        for c in range(count):
            rows = pl.ds(c * CHUNK, CHUNK)
            attn_in[rows, :] = (source[rows, :] * gain).astype(BF16)
    else:
        start_all(copies)
    wait_all(copies)
    mask_a, mask_b = lane_masks()
    blocks = block_mask()
    first = lax.broadcasted_iota(jnp.int32, (CHUNK, PAIR), 1) < HD
    causal = lax.broadcasted_iota(jnp.int32, (CHUNK, CHUNK), 0) >= lax.broadcasted_iota(
        jnp.int32, (CHUNK, CHUNK), 1
    )
    states = [None] * pairs
    for c in range(count):
        rows = pl.ds(c * CHUNK, CHUNK)
        proj = nn(attn_in[rows, :], weight[...])
        query, keys = proj[:, :width], proj[:, width : 2 * width]
        fq = jnp.where(query > 0, query + 1.0, jnp.exp(jnp.minimum(query, 0.0))).astype(BF16)
        fk = jnp.where(keys > 0, keys + 1.0, jnp.exp(jnp.minimum(keys, 0.0))).astype(BF16)
        val = proj[:, 2 * width :].astype(BF16)
        fq_out[rows, :] = fq
        fk_out[rows, :] = fk
        val_out[rows, :] = val
        for p in range(pairs):
            q, k, v = pair_of(fq, p), pair_of(fk, p), pair_of(val, p)
            v_a = v * mask_a + mask_b
            v_b = v * mask_b + mask_a
            s_a = jnp.where(causal, nt(q * mask_a, k), 0.0).astype(BF16)
            s_b = jnp.where(causal, nt(q * mask_b, k), 0.0).astype(BF16)
            r_a, r_b = nn(s_a, v_a), nn(s_b, v_b)
            if c > 0:
                high, low = split(states[p])
                past = nn(q, high) + nn(q, low)
                r_a = r_a + past[:, :PAIR]
                r_b = r_b + past[:, PAIR:]
            numer = jnp.where(first, r_a, r_b)
            denom = pltpu.roll(jnp.where(first, r_b, r_a), HD, axis=1)
            inverse = 1.0 / denom
            cols = pl.ds(p * PAIR, PAIR)
            att_out[rows, cols] = (numer * inverse).astype(BF16)
            rden_out[rows, cols] = inverse.astype(BF16)
            if c + 1 < count:
                new = tn(k, jnp.concatenate([v_a, v_b], 1)) * blocks
                states[p] = new if c == 0 else states[p] + new


def attn_fwd(meta, source, pieces, groups, position, count_vec):
    rows, full = source.shape
    width = full // groups
    n = len(pieces)
    shapes = [jax.ShapeDtypeStruct((rows, width), BF16)] * 5
    scratch = [pltpu.VMEM((full, 3 * width), BF16), pltpu.SemaphoreType.DMA((n,))]
    if count_vec:
        shapes += [
            jax.ShapeDtypeStruct((rows, full), BF16),
            jax.ShapeDtypeStruct((count_vec, full), F32),
        ]
        vec_rows = pieces[0].shape[0] - full // n
        scratch += [
            pltpu.VMEM((n, vec_rows, pieces[0].shape[1]), BF16),
            pltpu.SemaphoreType.DMA((n,)),
        ]
    return pl.pallas_call(
        functools.partial(attn_fwd_kernel, n, count_vec, position * 3 * width),
        out_shape=tuple(shapes),
        in_specs=[SMEM, VMEM] + [ANY] * n,
        out_specs=(VMEM,) * len(shapes),
        scratch_shapes=scratch,
        compiler_params=pltpu.CompilerParams(vmem_limit_bytes=VMEM_LIMIT),
        cost_estimate=cost(8, 6),
        name="attn_fwd",
    )(meta, source, *pieces)


def rest_copies(meta, which, pieces, dst, sems, groups):
    n = len(pieces)
    full = dst.shape[0]
    if which:
        hidden = dst.shape[1]
        cols = (full + (which - 1) * hidden, hidden)
        return piece_copies(meta[0], pieces, dst, sems.at[which], None, cols)
    width = full // groups
    if n == 1:
        found = []
        for j in range(groups):
            at = pl.multiple_of(lax.rem(meta[1] + j, groups) * width, width)
            found.append(
                pltpu.make_async_copy(
                    pieces[0].at[pl.ds(at, width), pl.ds(0, full)],
                    dst.at[pl.ds(j * width, width)],
                    sems.at[0, j],
                )
            )
        return found
    span = n // groups

    def turned(owner):
        group = lax.rem(owner // span - meta[1] + groups, groups)
        return group * span + lax.rem(owner, span)

    return piece_copies(meta[0], pieces, dst, sems.at[0], turned, (0, full))


def mlp_kernel(n_pieces, n_atts, groups, part, meta, *refs):
    atts = refs[:n_atts]
    tok, cot, vec, bias = refs[n_atts : n_atts + 4]
    pieces = refs[n_atts + 4 : n_atts + 4 + n_pieces]
    refs = refs[n_atts + 4 + n_pieces :]
    send_out, keep_out, hidden_out, gpre_out, min_out, resid_out = refs[:6]
    w_o, w_i, w_b, sems = refs[6:]
    i = pl.program_id(0)

    def loads(which):
        return rest_copies(meta, which, pieces, (w_o, w_i, w_b)[which], sems, groups)

    @pl.when(i == 0)
    def _():
        for which in range(3):
            start_all(loads(which))
        wait_all(loads(0))

    gain = vec[1:2, :]
    start = (2 * part + (i ^ (1 - meta[3]))) * CHUNK
    keep = keep_of(meta[2], start, CHUNK)
    g_low = (cot[...].astype(F32) * keep).astype(BF16)
    mixed = nn(jnp.concatenate([att[...] for att in atts], 1), w_o[...])
    resid = tok[...].astype(F32) + mixed
    resid_out[...] = resid
    normed, _ = normalize(resid)
    mlp_in = (normed * gain).astype(BF16)
    min_out[...] = mlp_in

    @pl.when(i == 0)
    def _():
        wait_all(loads(1))
        wait_all(loads(2))

    pre = nn(mlp_in, w_i[...]) + bias[...]
    square = pre * pre
    t = jnp.tanh(GELU_A * pre * (1.0 + GELU_B * square))
    half = 0.5 * (1.0 + t)
    hidden_out[...] = (pre * half).astype(BF16)
    slope = half + (0.5 * GELU_A) * pre * (1.0 - t * t) * (1.0 + (3.0 * GELU_B) * square)
    gpre = (nn(g_low, w_b[...]) * slope).astype(BF16)
    gpre_out[...] = gpre
    grad = nt(gpre, w_i[...]).astype(BF16)

    @pl.when(i == 0)
    def _():
        send_out[...] = grad

    @pl.when(i == 1)
    def _():
        keep_out[...] = grad


def mlp(meta, part, atts, groups, tokens, cotangent, vec, bias, pieces):
    n, n_atts = len(pieces), len(atts)
    rows = 2 * CHUNK
    width, hidden = tokens.shape[1], bias.shape[1]

    def rowed(cols, base):
        return pl.BlockSpec((CHUNK, cols), lambda i, m: (base + (i ^ (1 - m[3])), 0))

    def whole(shape):
        return pl.BlockSpec(shape, lambda i, m: (0, 0))

    shapes = [(CHUNK, width), (CHUNK, width), (rows, hidden), (rows, hidden), (rows, width)]
    return pl.pallas_call(
        functools.partial(mlp_kernel, n, n_atts, groups, part),
        out_shape=tuple(jax.ShapeDtypeStruct(shape, BF16) for shape in shapes)
        + (jax.ShapeDtypeStruct((rows, width), F32),),
        grid_spec=pltpu.PrefetchScalarGridSpec(
            num_scalar_prefetch=1,
            grid=(2,),
            in_specs=[rowed(a.shape[1], 2 * part) for a in atts]
            + [rowed(width, 2 * part)] * 2
            + [whole(vec.shape), whole(bias.shape)]
            + [ANY] * n,
            out_specs=(
                whole((CHUNK, width)),
                whole((CHUNK, width)),
                rowed(hidden, 0),
                rowed(hidden, 0),
                rowed(width, 0),
                rowed(width, 0),
            ),
            scratch_shapes=[
                pltpu.VMEM((width, width), BF16),
                pltpu.VMEM((width, hidden), BF16),
                pltpu.VMEM((width, hidden), BF16),
                pltpu.SemaphoreType.DMA((3, max(n, groups))),
            ],
        ),
        compiler_params=pltpu.CompilerParams(vmem_limit_bytes=VMEM_LIMIT),
        cost_estimate=cost(8, 16),
        name="mlp_fwd_bwd",
    )(meta, *atts, tokens, cotangent, vec, bias, *pieces)


def mlp_out_kernel(n_pieces, parts, meta, *refs):
    hiddens = refs[:parts]
    pieces = refs[parts : parts + n_pieces]
    send, keep, w_b, sems = refs[parts + n_pieces :]
    copies = rest_copies(meta, 2, pieces, w_b, sems, 1)
    start_all(copies)
    wait_all(copies)
    for c, out in enumerate((send, keep)):
        at = pl.multiple_of((c ^ (1 - meta[3])) * CHUNK, CHUNK)
        for r in range(parts):
            out[pl.ds(r * CHUNK, CHUNK), :] = nt(hiddens[r][pl.ds(at, CHUNK), :], w_b[...]).astype(
                BF16
            )


def mlp_out(meta, hiddens, pieces, width):
    n, parts = len(pieces), len(hiddens)
    hidden = hiddens[0].shape[1]
    return pl.pallas_call(
        functools.partial(mlp_out_kernel, n, parts),
        out_shape=(jax.ShapeDtypeStruct((parts * CHUNK, width), BF16),) * 2,
        in_specs=[SMEM] + [VMEM] * parts + [ANY] * n,
        out_specs=(VMEM,) * 2,
        scratch_shapes=[
            pltpu.VMEM((width, hidden), BF16),
            pltpu.SemaphoreType.DMA((3, n)),
        ],
        compiler_params=pltpu.CompilerParams(vmem_limit_bytes=VMEM_LIMIT),
        cost_estimate=cost(4, 8),
        name="mlp_out",
    )(meta, *hiddens, *pieces)


def offset_of(n_blocks, base, k, size):
    return pl.multiple_of((base ^ k) * size, size) if n_blocks == PAIRED else k * size


def spread(n_blocks, base, scratch, own, sib, start):
    size = own.shape[1]
    cols = pl.ds(start, scratch.shape[1])
    for k in range(n_blocks):
        at = offset_of(n_blocks, base, k, size)
        (own, sib)[k & 1][k >> 1, :, cols] = scratch[pl.ds(at, size), :]


def mlp_grads_kernel(n_blocks, parts, meta, *refs):
    hiddens, gpres, mins = (refs[a * parts : (a + 1) * parts] for a in range(3))
    cot = refs[3 * parts]
    own, sib, bin_out, bback_out, scratch, g_low = refs[3 * parts + 1 :]
    rows = hiddens[0].shape[0]
    total_in = total_back = None
    for r in range(parts):
        keep = keep_of(meta[2], r * rows, rows)
        g = cot[pl.ds(r * rows, rows), :].astype(F32) * keep
        g_low[pl.ds(r * rows, rows), :] = g.astype(BF16)
        back = jnp.sum(g, 0, keepdims=True)
        inner = jnp.sum(gpres[r][...].astype(F32), 0, keepdims=True)
        total_in = inner if total_in is None else total_in + inner
        total_back = back if total_back is None else total_back + back
    bin_out[...] = total_in
    bback_out[...] = total_back
    step = 256
    hidden = hiddens[0].shape[1]
    for s in range(scratch.shape[0] // step):
        cols = pl.ds(s * step, step)
        up = down = None
        for r in range(parts):
            part = tn(mins[r][:, cols], gpres[r][...])
            up = part if up is None else up + part
            part = tn(g_low[pl.ds(r * rows, rows), cols], hiddens[r][...])
            down = part if down is None else down + part
        scratch[cols, pl.ds(0, hidden)] = up.astype(BF16)
        scratch[cols, pl.ds(hidden, hidden)] = down.astype(BF16)
    spread(n_blocks, meta[0], scratch, own, sib, 0)


def mlp_grads(meta, n_blocks, hiddens, gpres, mins, cotangent):
    parts = len(hiddens)
    hidden, width = hiddens[0].shape[1], mins[0].shape[1]
    blocks = jax.ShapeDtypeStruct((n_blocks // 2, width // n_blocks, 2 * hidden), BF16)
    return pl.pallas_call(
        functools.partial(mlp_grads_kernel, n_blocks, parts),
        out_shape=(
            blocks,
            blocks,
            jax.ShapeDtypeStruct((1, hidden), F32),
            jax.ShapeDtypeStruct((1, width), F32),
        ),
        in_specs=[SMEM] + [VMEM] * (3 * parts + 1),
        out_specs=(VMEM,) * 4,
        scratch_shapes=[
            pltpu.VMEM((width, 2 * hidden), BF16),
            pltpu.VMEM(cotangent.shape, BF16),
        ],
        compiler_params=pltpu.CompilerParams(vmem_limit_bytes=VMEM_LIMIT),
        cost_estimate=cost(8, 16),
        name="mlp_grads",
    )(meta, *hiddens, *gpres, *mins, cotangent)


def norm_bwd_kernel(parts, meta, *refs):
    totals = refs[: 2 * parts]
    resids = refs[2 * parts : 3 * parts]
    cot, vec, gres_out, gmix_out, gain_out = refs[3 * parts :]
    i = pl.program_id(0)
    chunk = 2 * (i // 2) + (lax.rem(i, 2) ^ meta[3])
    keep = keep_of(meta[2], chunk * CHUNK, CHUNK)

    @pl.when(i == 0)
    def _():
        gain_out[...] = jnp.zeros_like(gain_out)

    for r in range(parts):
        for h in range(2):

            @pl.when(i == 2 * r + h)
            def _():
                grad = totals[2 * r + h][...].astype(F32)
                normed, factor = normalize(resids[r][...])
                gain_out[...] += jnp.sum(grad * normed, 0, keepdims=True)
                gres = cot[...].astype(F32) * keep + norm_back(
                    grad * vec[1:2, :], normed, factor
                )
                gres_out[...] = gres
                gmix_out[...] = gres.astype(BF16)


def norm_bwd(meta, totals, resids, cotangent, vec):
    parts = len(resids)
    rows, full = cotangent.shape

    def whole(shape):
        return pl.BlockSpec(shape, lambda i, m: (0, 0))

    def inner(r):
        def index(i, m):
            bit = lax.rem(jnp.clip(i - 2 * r, 0, 1), 2)
            return (bit ^ m[3], 0)

        return pl.BlockSpec((CHUNK, full), index)

    rowed = pl.BlockSpec((CHUNK, full), lambda i, m: (2 * (i // 2) + (lax.rem(i, 2) ^ m[3]), 0))
    return pl.pallas_call(
        functools.partial(norm_bwd_kernel, parts),
        out_shape=(
            jax.ShapeDtypeStruct((rows, full), F32),
            jax.ShapeDtypeStruct((rows, full), BF16),
            jax.ShapeDtypeStruct((1, full), F32),
        ),
        grid_spec=pltpu.PrefetchScalarGridSpec(
            num_scalar_prefetch=1,
            grid=(2 * parts,),
            in_specs=[whole(t.shape) for t in totals]
            + [inner(r) for r in range(parts)]
            + [rowed, whole(vec.shape)],
            out_specs=(rowed, rowed, whole((1, full))),
        ),
        compiler_params=pltpu.CompilerParams(vmem_limit_bytes=VMEM_LIMIT),
        cost_estimate=cost(1, 16),
        name="norm_bwd",
    )(meta, *totals, *resids, cotangent, vec)


def group_rows(meta, group, width, pieces, dst, sems, start):
    full = dst.shape[1]
    if len(pieces) == 1:
        at = pl.multiple_of(group * width, width)
        copy = pltpu.make_async_copy(
            pieces[0].at[pl.ds(at, width), pl.ds(0, full)], dst, sems.at[0]
        )
        return copy.start() if start else copy.wait()
    size = pieces[0].shape[0]
    for part in range(width // size):
        wanted = group * (width // size) + part
        target = dst.at[pl.ds(part * size, size)]
        if not start:
            pltpu.make_async_copy(
                pieces[0].at[:, pl.ds(0, full)], target, sems.at[part]
            ).wait()
            continue
        for k, piece in enumerate(pieces):

            @pl.when(wanted == owner_of(meta[0], k))
            def _():
                pltpu.make_async_copy(
                    piece.at[:, pl.ds(0, full)], target, sems.at[part]
                ).start()


def attn_bwd_kernel(shape, meta, *refs):
    n, groups, position, start, n_atts, n_vectors, n_blocks = shape
    is_first, is_last = position == 0, position == groups - 1
    refs = list(refs)

    def take(count):
        found = refs[:count]
        del refs[:count]
        return found

    gmix, fq, fk, val, att, rden = take(6)
    (acc_in,) = take(1) if not is_first else (None,)
    attn_in, *atts = take(1 + n_atts) if is_first else (None,)
    tok, gres, vec, *vectors = take(3 + n_vectors) if is_last else (None, None, None)
    pieces_o, pieces_w = take(n), take(n)
    (acc_out,) = take(1)
    own, sib = take(2) if is_first or is_last else (None, None)
    w_o, w_q, state_scr, later, sems_o, sems_w = take(6)
    width = fq.shape[1]
    pairs = width // PAIR
    full = gmix.shape[1]
    i = pl.program_id(0)
    count = fk.shape[0] // CHUNK
    c = count - 1 - i
    place = meta[1]
    group = lax.rem(place + position, groups)
    mask_a, mask_b = lane_masks()
    blocks = block_mask()

    def weight_copies():
        return piece_copies(meta[0], pieces_w, w_q, sems_w, None, (start, 3 * width))

    def side_copies():
        found = [pltpu.make_async_copy(attn_in, ain_scr, side_sems.at[0])]
        for a in range(n_atts):
            found.append(
                pltpu.make_async_copy(
                    atts[a], att_scr.at[:, pl.ds(a * width, width)], side_sems.at[a + 1]
                )
            )
        return found

    if is_first:
        gproj_scr, gcol_scr, ain_scr, att_scr, product, side_sems = take(6)
    if is_last:
        (gain_scr,) = take(1)

    @pl.when(i == 0)
    def _():
        group_rows(meta, group, width, pieces_o, w_o, sems_o, True)
        start_all(weight_copies())
        if is_first:
            start_all(side_copies())
        if is_last:
            gain_scr[...] = jnp.zeros_like(gain_scr)
        later[...] = jnp.zeros_like(later)
        for p in range(pairs):
            state = jnp.zeros((PAIR, 2 * PAIR), F32)
            for s in range(count):
                high, low = split(state)
                state_scr[s, p, 0] = high
                state_scr[s, p, 1] = low
                if s + 1 < count:
                    rows, cols = pl.ds(s * CHUNK, CHUNK), pl.ds(p * PAIR, PAIR)
                    v = val[rows, cols]
                    aug = jnp.concatenate([v * mask_a + mask_b, v * mask_b + mask_a], 1)
                    state = state + tn(fk[rows, cols], aug) * blocks
        group_rows(meta, group, width, pieces_o, w_o, sems_o, False)
        wait_all(weight_copies())

    first = lax.broadcasted_iota(jnp.int32, (CHUNK, PAIR), 1) < HD
    row = lax.broadcasted_iota(jnp.int32, (CHUNK, CHUNK), 0)
    col = lax.broadcasted_iota(jnp.int32, (CHUNK, CHUNK), 1)
    causal, causal_t = row >= col, row <= col
    head_row = lax.broadcasted_iota(jnp.int32, (width, width), 0) // HD
    head_col = lax.broadcasted_iota(jnp.int32, (width, width), 1) // HD
    head_sum = (head_row == head_col).astype(F32).astype(BF16)
    rows = pl.ds(pl.multiple_of(c * CHUNK, CHUNK), CHUNK)
    grad_att = nt(gmix[...], w_o[...])
    inverse = rden[...].astype(F32)
    gnum = (grad_att * inverse).astype(BF16)
    dots = nn((grad_att * att[...].astype(F32)).astype(BF16), head_sum)
    gden = (-dots * inverse).astype(BF16).astype(F32)
    found_q, found_k, found_v = [], [], []
    for p in range(pairs):
        cols = pl.ds(p * PAIR, PAIR)
        q, k, v = fq[:, cols], fk[rows, cols], val[rows, cols]
        num = pair_of(gnum, p)
        den = (pltpu.roll(pair_of(gden, p), HD, axis=1) * (1.0 / HD)).astype(BF16)
        n_a, n_b = num * mask_a + den * mask_b, num * mask_b + den * mask_a
        q_a, q_b = q * mask_a, q * mask_b
        v_a, v_b = v * mask_a + mask_b, v * mask_b + mask_a
        n_cat = jnp.concatenate([n_a, n_b], 1)
        v_cat = jnp.concatenate([v_a, v_b], 1)
        st_a = jnp.where(causal_t, nt(k, q_a), 0.0).astype(BF16)
        st_b = jnp.where(causal_t, nt(k, q_b), 0.0).astype(BF16)
        gs_a = jnp.where(causal, nt(n_a, v_a), 0.0).astype(BF16)
        gs_b = jnp.where(causal, nt(n_b, v_b), 0.0).astype(BF16)
        gt_a = jnp.where(causal_t, nt(v_a, n_a), 0.0).astype(BF16)
        gt_b = jnp.where(causal_t, nt(v_b, n_b), 0.0).astype(BF16)
        high, low = split(later[p])
        past = nn(k, high) + nn(k, low)
        gq = nn(gs_a, k * mask_a) + nn(gs_b, k * mask_b)
        gq = gq + nt(n_cat, state_scr[c, p, 0]) + nt(n_cat, state_scr[c, p, 1])
        gk = nn(gt_a, q_a) + nn(gt_b, q_b) + nt(v_cat, high) + nt(v_cat, low)
        gv = nn(st_a, num * mask_a) + nn(st_b, num * mask_b)
        gv = gv + jnp.where(first, past[:, :PAIR], past[:, PAIR:])
        later[p] = later[p] + tn(q, n_cat) * blocks
        found_q.append((gq * jnp.minimum(q.astype(F32), 1.0)).astype(BF16))
        found_k.append((gk * jnp.minimum(k.astype(F32), 1.0)).astype(BF16))
        found_v.append(gv.astype(BF16))
    gproj = jnp.concatenate(found_q + found_k + found_v, 1)
    grad = nt(gproj, w_q[...])
    if not is_first:
        grad = grad + acc_in[...]
    if not is_last:
        acc_out[...] = grad
    else:
        normed, factor = normalize(tok[...].astype(F32))
        gain_scr[...] += jnp.sum(grad * normed, 0, keepdims=True)
        acc_out[...] = gres[...] + norm_back(grad * vec[0:1, :], normed, factor)

        @pl.when(i == count - 1)
        def _():
            for a, source in enumerate([gain_scr] + vectors):
                size = source.shape[1] // n_blocks
                for k in range(n_blocks):
                    at = offset_of(n_blocks, meta[0], k, size)
                    (own, sib)[k & 1][k >> 1, a : a + 1, pl.ds(0, size)] = source[
                        :, pl.ds(at, size)
                    ]

    if is_first:
        gproj_scr[rows, :] = gproj
        gcol_scr[rows, :] = gmix[:, pl.ds(pl.multiple_of(place * width, width), width)]

        @pl.when(i == count - 1)
        def _():
            wait_all(side_copies())
            for s in range(full // 256):
                piece = pl.ds(s * 256, 256)
                product[piece, pl.ds(0, 3 * width)] = tn(
                    ain_scr[:, s * 256 : (s + 1) * 256], gproj_scr[...]
                ).astype(BF16)
            for j in range(groups):
                at = pl.multiple_of(lax.rem(place + j, groups) * width, width)
                product[pl.ds(at, width), pl.ds(3 * width, width)] = tn(
                    att_scr[:, j * width : (j + 1) * width], gcol_scr[...]
                ).astype(BF16)
            spread(n_blocks, meta[0], product, own, sib, 0)


def attn_bwd(meta, n_blocks, position, start, gmix, heads, pieces_o, pieces_w, extra):
    n = len(pieces_o)
    rows, full = gmix.shape
    width = heads[0].shape[1]
    groups = full // width
    count = rows // CHUNK
    is_first, is_last = position == 0, position == groups - 1

    def rowed(cols):
        return pl.BlockSpec((CHUNK, cols), lambda i: (count - 1 - i, 0))

    def whole(shape):
        return pl.BlockSpec(shape, lambda i: (0,) * len(shape))

    specs = [rowed(full), rowed(width), whole((rows, width)), whole((rows, width))]
    specs += [rowed(width), rowed(width)]
    n_atts = n_vectors = 0
    if is_first:
        n_atts = len(extra) - 1
        specs += [ANY] * len(extra)
    else:
        specs += [rowed(full)]
    if is_last:
        n_vectors = len(extra) - 4
        specs += [rowed(full), rowed(full)] + [whole(v.shape) for v in extra[3:]]
    shapes, outs = [jax.ShapeDtypeStruct((rows, full), F32)], [rowed(full)]
    scratch = [
        pltpu.VMEM((width, full), BF16),
        pltpu.VMEM((full, 3 * width), BF16),
        pltpu.VMEM((count, width // PAIR, 2, PAIR, 2 * PAIR), BF16),
        pltpu.VMEM((width // PAIR, PAIR, 2 * PAIR), F32),
        pltpu.SemaphoreType.DMA((max(1, width * n // full),)),
        pltpu.SemaphoreType.DMA((n,)),
    ]
    if is_first:
        blocks = (n_blocks // 2, full // n_blocks, 4 * width)
        shapes += [jax.ShapeDtypeStruct(blocks, BF16)] * 2
        outs += [whole(blocks)] * 2
        scratch += [
            pltpu.VMEM((rows, 3 * width), BF16),
            pltpu.VMEM((rows, width), BF16),
            pltpu.VMEM((rows, full), BF16),
            pltpu.VMEM((rows, full), BF16),
            pltpu.VMEM((full, 4 * width), BF16),
            pltpu.SemaphoreType.DMA((n_atts + 1,)),
        ]
    if is_last:
        small = (n_blocks // 2, 4, full // n_blocks)
        shapes += [jax.ShapeDtypeStruct(small, F32)] * 2
        outs += [whole(small)] * 2
        scratch += [pltpu.VMEM((1, full), F32)]
    shape = (n, groups, position, start, n_atts, n_vectors, n_blocks)
    return pl.pallas_call(
        functools.partial(attn_bwd_kernel, shape),
        grid=(count,),
        out_shape=tuple(shapes),
        in_specs=[SMEM] + specs + [ANY] * (2 * n),
        out_specs=tuple(outs),
        scratch_shapes=scratch,
        compiler_params=pltpu.CompilerParams(vmem_limit_bytes=VMEM_LIMIT),
        cost_estimate=cost(10, 7),
        name="attn_bwd",
    )(meta, gmix, *heads, *extra, *pieces_o, *pieces_w)


def finish_kernel(parts, meta, *refs):
    resids = refs[:parts]
    kept, other, vec, out = refs[parts:]
    bias = vec[3:4, :]
    for r in range(parts):
        for source, h in ((kept, 0), (other, 1)):
            inner = pl.multiple_of((h ^ meta[3]) * CHUNK, CHUNK)
            at = pl.multiple_of(r * 2 * CHUNK + inner, CHUNK)
            summed = source[pl.ds(r * CHUNK, CHUNK), :].astype(F32)
            total = resids[r][pl.ds(inner, CHUNK), :] + (summed + bias)
            keep = keep_of(meta[2], at, CHUNK)
            out[pl.ds(at, CHUNK), :] = (total * keep).astype(BF16)


def finish(meta, resids, kept, other, vec):
    rows, width = 2 * CHUNK * len(resids), kept.shape[1]
    return pl.pallas_call(
        functools.partial(finish_kernel, len(resids)),
        out_shape=jax.ShapeDtypeStruct((rows, width), BF16),
        in_specs=[SMEM] + [VMEM] * (len(resids) + 3),
        out_specs=VMEM,
        compiler_params=pltpu.CompilerParams(vmem_limit_bytes=VMEM_LIMIT),
        cost_estimate=cost(0.01, 8),
        name="finish",
    )(meta, *resids, kept, other, vec)


def assemble_kernel(groups, turned, meta, *refs):
    pieces, (qkv, out) = refs[:-2], refs[-2:]
    width = out.shape[1] // groups
    for d, piece in enumerate(pieces):
        group = meta[1] ^ d if turned else d
        for t in range(4):
            value = piece[:, pl.ds(t * width, width)].astype(F32)
            start = t % 3 * groups * width + group * width
            at = pl.ds(pl.multiple_of(start, width), width)
            (out if t == 3 else qkv)[:, at] = value


def assemble(meta, groups, turned, pieces):
    rows, width = pieces[0].shape[0], pieces[0].shape[1] // 4
    return pl.pallas_call(
        functools.partial(assemble_kernel, groups, turned),
        out_shape=(
            jax.ShapeDtypeStruct((rows, 3 * groups * width), F32),
            jax.ShapeDtypeStruct((rows, groups * width), F32),
        ),
        in_specs=[SMEM] + [VMEM] * len(pieces),
        out_specs=(VMEM,) * 2,
        compiler_params=pltpu.CompilerParams(vmem_limit_bytes=VMEM_LIMIT),
        cost_estimate=cost(0.01, 3),
        name="assemble",
    )(meta, *pieces)


def send(arr, move):
    return lax.ppermute(arr, "dp", [(i, move(i)) for i in range(PAIRED)])


def near(i):
    return i ^ (4 if i & 1 else 2)


def far(i):
    return i ^ (2 if i & 1 else 4)


def across(i):
    return i ^ 1


def after(arrs, *deps):
    return lax.optimization_barrier((arrs, deps))[0]


def gather_pieces(arr):
    one, two = send(arr, near), send(arr, far)
    three = send(one, far)
    pieces = []
    for piece in (arr, one, two, three):
        pieces += [piece, send(piece, across)]
    return pieces


def chip_sum(own, sib):
    return own.astype(F32) + send(sib, across).astype(F32)


def plane_sum(both, kind):
    total = both[0]
    for k in range(1, PAIRED // 2):
        moved = send(both[k].astype(kind), lambda i, k=k: i ^ (2 * k))
        total = total + moved.astype(F32)
    return total


def swapped(arr, bits):
    return lax.ppermute(arr, "mp", [(i, i ^ bits) for i in range(4)])


def add_low(left, right):
    return (left.astype(F32) + right.astype(F32)).astype(BF16)


def per_device(
    n_dp, n_mp, tokens, lengths, w_qkv, w_out, ln1_gain, ln2_gain, w_in, b_in, w_back, b_back,
    cotangent,
):
    rows, full = tokens.shape
    groups = n_mp
    per = 2
    paired = n_dp == PAIRED and n_mp == 4
    index = lax.axis_index("dp").astype(jnp.int32)
    place = lax.axis_index("mp").astype(jnp.int32)
    zero = jnp.zeros_like(index)
    meta = jnp.stack(
        [index if paired else zero, place, lengths[0], (place & 1) if paired else zero]
    )
    vectors = [v[None] for v in (ln1_gain, ln2_gain, b_in, b_back)]

    def gather(arr, axis=0):
        return lax.all_gather(arr, "dp", axis=axis, tiled=True)

    first_sent = prep_first(
        meta, groups, per, 16 if paired else 0, w_qkv, vectors if paired else ()
    )
    normed_one, _ = normalize(tokens.astype(F32))
    parts = rows // (2 * CHUNK)
    found, totals = [None] * parts, [None] * (2 * parts)

    if not paired:
        sent = [first_sent] + list(prep_rest(meta, groups, per, w_qkv, w_out, w_in, w_back))
        gathered = [[gather(arr)] for arr in sent]
        bundles, rest = gathered[:-1], gathered[-1]
        gain_one, gain_two, bias, bias_back = (gather(v, 1) for v in vectors)
        attn_in = (normed_one * gain_one).astype(BF16)
        vec = jnp.concatenate([gain_one, gain_two, gain_two, bias_back], 0)
        heads = [
            attn_fwd(meta, attn_in, bundles[j // per], groups, j % per, 0) for j in range(groups)
        ]
    else:
        bundles = [gather_pieces(first_sent)]
        raw = after((w_qkv, w_out, w_in, w_back), bundles[0][1])
        second, third = prep_rest(meta, groups, per, *raw)
        bundles.append(gather_pieces(second))
        rest = gather_pieces(after(third, bundles[0][2]))
        heads = [attn_fwd(meta, normed_one, bundles[0], groups, 0, 4)]
        attn_in, vec = heads[0][5:]
        bias = vec[2:3]
        heads.append(attn_fwd(meta, attn_in, bundles[0], groups, 1, 0))
        attn_in = after(attn_in, rest[2])
        heads.append(attn_fwd(meta, attn_in, bundles[1], groups, 0, 0))
        heads.append(attn_fwd(meta, attn_in, bundles[1], groups, 1, 0))
    heads = [h[:5] for h in heads]
    atts = [h[3] for h in heads]

    for r in reversed(range(parts)):
        found[r] = mlp(meta, r, atts, groups, tokens, cotangent, vec, bias, rest)
    aways, keeps, hiddens, gpres, mins, resids = (list(x) for x in zip(*found))
    if paired:
        pairs = [None] * parts
        for r in reversed(range(parts)):
            pairs[r] = add_low(keeps[r], swapped(aways[r], 1))
        for r in reversed(range(parts)):
            totals[2 * r] = add_low(pairs[r], swapped(pairs[r], 2))
            totals[2 * r + 1] = swapped(totals[2 * r], 1)
    wide_own, wide_sib, g_bin, g_bback = mlp_grads(meta, n_dp, hiddens, gpres, mins, cotangent)
    out_away, out_kept = mlp_out(meta, hiddens, rest, full)

    def stacked_sum(own, sib):
        both = jnp.stack([own, sib], 1).reshape((n_dp,) + own.shape[1:])
        return lax.psum_scatter(both.astype(F32), "dp", scatter_dimension=0)

    def mp_sum(arr):
        return lax.psum(arr.astype(F32), "mp").astype(BF16)

    if not paired:
        for r in range(parts):
            totals[2 * r], totals[2 * r + 1] = mp_sum(keeps[r]), mp_sum(aways[r])
        out_sums = mp_sum(out_kept), mp_sum(out_away)
        grads = stacked_sum(wide_own, wide_sib)
    else:
        out_pair = add_low(out_kept, swapped(after(out_away, pairs[0]), 1))
        totals = after(totals, out_pair)
        got = send(wide_sib, across)

    def column(j):
        return bundles[j // per], j % per * 3 * (full // groups)

    gres, gmix, g_gain2 = norm_bwd(meta, totals, resids, cotangent, vec)
    acc, own, sib = attn_bwd(
        meta, n_dp, 0, column(0)[1], gmix, heads[0], rest, column(0)[0], (attn_in, *atts)
    )
    if paired:
        out_total = add_low(out_pair, swapped(out_pair, 2))
        both = chip_sum(own, after(sib, out_total))
        gmix = after(gmix, both)
        piece = plane_sum(both, BF16).astype(BF16)
        out_sums = out_total, swapped(out_total, 1)
        second = swapped(piece, 2)
        pieces = [piece, swapped(piece, 1), second, swapped(second, 1)]
        away = after(add_low(wide_own[1::2], got[1::2]), piece)
        kept = wide_own[::2].astype(F32) + got[::2].astype(F32)
        kept = kept + send(away, lambda i: i ^ 2).astype(F32)
        low = after(kept[1].astype(BF16), second)
        grads = kept[0] + send(low, lambda i: i ^ 4).astype(F32)
    else:
        every = lax.all_gather(stacked_sum(own, sib).astype(BF16), "mp")
        pieces = [every[d] for d in range(groups)]
    grad_qkv, grad_out = assemble(meta, groups, paired, pieces)
    for j in range(1, groups - 1):
        if paired and j == groups - 2:
            gmix = after(gmix, piece, out_total)
        (acc,) = attn_bwd(
            meta, n_dp, j, column(j)[1], gmix, heads[j], rest, column(j)[0], (acc,)
        )
    j = groups - 1
    if paired:
        gmix = after(gmix, second)
    grad_tokens, own, sib = attn_bwd(
        meta, n_dp, j, column(j)[1], gmix, heads[j], rest, column(j)[0],
        (acc, tokens, gres, vec, g_gain2, g_bback, g_bin),
    )
    if paired:
        small = plane_sum(chip_sum(own, after(sib, out_sums, pieces)), F32)
    else:
        small = stacked_sum(own, sib)
    output = finish(meta, resids, *out_sums, after(vec, acc))
    hidden = w_in.shape[1]
    grad_in, grad_back = grads[:, :hidden], grads[:, hidden:].T
    return (
        output, grad_tokens, grad_qkv, grad_out, small[0], small[1], grad_in,
        small[3, : b_in.shape[0]], grad_back, small[2],
    )


def solution(mesh):
    in_specs = (
        P("dp", None),
        P("dp"),
        P("dp", None),
        P("dp", None),
        P("dp"),
        P("dp"),
        P("dp", "mp"),
        P(("mp", "dp")),
        P("mp", "dp"),
        P("dp"),
        P("dp", None),
    )
    out_specs = (
        P("dp", None),
        P("dp", None),
        P("dp", None),
        P("dp", None),
        P("dp"),
        P("dp"),
        P("dp", "mp"),
        P(("mp", "dp")),
        P("mp", "dp"),
        P("dp"),
    )
    body = functools.partial(per_device, mesh.shape["dp"], mesh.shape["mp"])
    return jax.shard_map(
        body, mesh=mesh, in_specs=in_specs, out_specs=out_specs, check_vma=False
    )
```
